32 devices in a mesh: groups: 1, dp: 32 (over z, y, x, core).
Axes of the slice: x: 2, y: 2, z: 4, core: 2. Of those that a mesh axis runs over, the one named last changes fastest.
Arguments:
- residual: bfloat16 [512, 4096], P(('groups', 'dp')), may hold values from -11 to 11
- queries: bfloat16 [512, 8192], P(('groups', 'dp')), may hold values from -160 to 160
- new_kv: bfloat16 [2, 512, 512], P(None, ('groups', 'dp')), may hold values from -6 to 6
- cache_kv: bfloat16 [2, 512, 128, 512], P(None, ('groups', 'dp')), may hold values from -7 to 7
- lengths: int32 [512], P(('groups', 'dp')), may hold values from 2 to 128, as said below
- out_weight: bfloat16 [8192, 4096], P('dp'), may hold values from -0.0625 to 0.0625
- norm_gain: float32 [4096], replicated, may hold values from 0.1 to 1.9
- w_gate: bfloat16 [32, 4096, 768], P('dp'), may hold values from -0.09375 to 0.09375
- w_up: bfloat16 [32, 4096, 768], P('dp'), may hold values from -0.09375 to 0.09375
- w_down: bfloat16 [32, 768, 4096], P('dp'), may hold values from -0.15625 to 0.15625
- expert_ids: int32 [512, 8], P(('groups', 'dp')), may hold values from 0 to 15, all different within a row; in each aligned block of 16 rows (0 to 15, 16 to 31, ...) at most 16 rows name the same one
- combine_weights: float32 [512, 8], P(('groups', 'dp')), may hold values from 0.05 to 0.3
Outputs:
- layer_out: bfloat16 [512, 4096], P(('groups', 'dp'))
The draws below stay inside these ranges and needn't reach their ends.
Inputs may be any that keep to these rules, and one draw needn't show every extreme that they name: `expert_ids`: in the 16 rows of each device no expert is named more than 16 times, a bound that some block reaches. Sequence t attends to cached positions 0 to lengths[t] - 1; some sequence uses all 128.
All inputs are finite; a program needn't handle non-finite values.
Results may differ from the reference program's by a relative error of at most 0.028.
Values may be sent and summed in bfloat16 or wider, within the bound.
No kernel may reach another device: no remote copies, remote signals or barrier semaphores. Data moves between devices by JAX's collectives and lax.ppermute only.
A program may use at most 128 MiB of HBM per device.

```python
import math
import jax
import jax.numpy as jnp
import numpy as np
from jax import lax

D = 4096
H = 64
KVH = 4
DH = 128
FF = 1536
TOP = 8
TOK_DEV = 16
CACHE = 128
TOKENS = 512
EXPERTS = 16
CAP = 16
N_DP = 32


def shared_keys(key):
    return jnp.clip(jax.random.normal(key, (TOKENS, CACHE, KVH * DH), jnp.float32), -6.0, 6.0)


def draw_cache_kv(key, part):
    cached_keys = shared_keys(key)
    key = jax.random.fold_in(key, 3)
    cached_values = jnp.clip(jax.random.normal(key, (TOKENS, CACHE, KVH * DH), jnp.float32), -6.0, 6.0)
    return jnp.stack([cached_keys, cached_values]).astype(jnp.bfloat16)


def draw_queries(key, part):
    key = jax.random.fold_in(key, 5)
    return jnp.clip(jax.random.normal(key, (TOKENS, H * DH), jnp.float32), -6.0, 6.0).astype(jnp.bfloat16)


def draw_lengths(key, part):
    key = jax.random.fold_in(key, 7)
    drawn = jax.random.randint(key, (TOKENS,), 2, CACHE + 1, jnp.int32)
    return drawn.at[0].set(CACHE)


def draw_residual(key, part):
    key = jax.random.fold_in(key, 9)
    base_key, row_key, column_key = jax.random.split(key, 3)
    base = jnp.clip(jax.random.normal(base_key, (TOKENS, D), jnp.float32), -6.0, 6.0)
    row_scale = jnp.exp(jax.random.uniform(row_key, (TOKENS, 1), jnp.float32, math.log(0.3), math.log(3.0)))
    column_scale = jnp.exp(jax.random.uniform(column_key, (1, D), jnp.float32, math.log(0.3), math.log(3.0)))
    return (0.2 * base * row_scale * column_scale).astype(jnp.bfloat16)


def block_scale(key, extent, pieces, smallest, top_value):
    factor_of = 1.0
    for axis_at, parts in pieces:
        draws = jax.random.uniform(jax.random.fold_in(jax.random.fold_in(key, 6), axis_at), (parts,), jnp.float32, smallest / len(pieces), top_value / len(pieces))
        factor_of = factor_of * jnp.repeat(jnp.exp(draws), extent[axis_at] // parts).reshape((-1,) + (1,) * (len(extent) - 1 - axis_at))
    return factor_of


def shared_out(stream_key, own, number, rows, number_of, top, most, slope):
    sequence = jax.random.permutation(stream_key, number_of)
    crowded, ordinary = load_shares(number_of, rows * top, most, slope, True), load_shares(number_of, rows * top, most, slope, False)
    places = jnp.arange(number_of)

    def named(sizes, rotation):
        used = int((sizes > 0).sum())
        fixed = max(1, used // 4)
        passed = fixed + (places - fixed + rotation * (used - fixed)) % max(1, number_of - fixed)
        return jnp.zeros((number_of,), jnp.int32).at[sequence[jnp.where(places < fixed, places, passed)]].set(jnp.asarray(sizes, jnp.int32))

    sizes = jnp.where(number % 4 == 0, named(crowded, number // 4), named(ordinary, number - number // 4 - 1))
    mixed = jax.random.permutation(jax.random.fold_in(own, 3), number_of)
    source_of, sink = mixed[0:number_of // 2 * 2:2], mixed[1:number_of // 2 * 2:2]
    room = jnp.minimum(sizes[source_of] - 1, most - sizes[sink]) // 2
    room = jnp.where((source_of == sequence[0]) | (sink == sequence[0]) | (sizes[sink] == 0), 0, jnp.maximum(room, 0))
    passed = jax.random.randint(jax.random.fold_in(own, 4), (number_of // 2,), 0, 1 << 20) % (room + 1)
    sizes = sizes.at[source_of].add(-passed).at[sink].add(passed)
    items = jnp.searchsorted(jnp.cumsum(sizes), jnp.arange(rows * top), side="right").astype(jnp.int32)
    listing = items.reshape(top, rows).T
    listing = listing[jax.random.permutation(jax.random.fold_in(own, 1), rows)]
    rotation = jax.random.randint(jax.random.fold_in(own, 2), (rows, 1), 0, top)
    return jnp.take_along_axis(listing, (jnp.arange(top)[None, :] + rotation) % top, axis=1)


def load_shares(number_of, total, bound, slope, full):
    portions = [(1 << 20) // math.isqrt(rank ** slope) + 1 for rank in range(1, number_of + 1)]
    largest = bound if full else min(bound, max(-(-total // number_of), total * portions[0] // sum(portions)))
    least = 1 if total - largest >= number_of - 1 else 0
    counts, spare = [largest] + [least] * (number_of - 1), total - largest - least * (number_of - 1)
    while spare > 0:
        candidates = [i for i in range(1, number_of) if counts[i] < largest] or [i for i in range(1, number_of) if counts[i] < bound]
        pool, budget = sum([portions[i] for i in candidates]), spare
        for i in candidates:
            addition = min(bound - counts[i], max(1, budget * portions[i] // pool), spare)
            counts[i] = counts[i] + addition
            spare = spare - addition
    return np.array(counts)


def gaussian(rng, dims, deviation, reach, shards=(), kind=jnp.bfloat16):
    gain = block_scale(rng, dims, shards, -0.22, 0.18) if shards else 1.0
    result = jax.random.normal(rng, dims, jnp.float32) * deviation * gain
    return jnp.minimum(jnp.maximum(result, -reach), reach).astype(kind)


def setup_inputs(seed: int = 0, part: int = 0) -> dict:
    key_of = jax.random.split(jax.random.key(seed), 13)
    part_keys = jax.random.split(jax.random.fold_in(key_of[12], part), 13)
    residual = draw_residual(jax.random.fold_in(jax.random.fold_in(key_of[12], part), 71), part)
    queries = draw_queries(jax.random.fold_in(jax.random.fold_in(key_of[12], part), 71), part)
    new_kv = gaussian(part_keys[2], (2, TOKENS, KVH * DH), 1.0, 6.0, ((1, 32),))
    cache_kv = draw_cache_kv(jax.random.fold_in(jax.random.fold_in(key_of[12], part), 71), part)
    lengths = draw_lengths(jax.random.fold_in(jax.random.fold_in(key_of[12], part), 71), part)
    out_weight = gaussian(key_of[5], (H * DH, D), (H * DH) ** -0.5, 0.0625, ((0, 32),))
    norm_gain = jnp.clip(1.0 + 0.18 * jax.random.normal(key_of[6], (D,), jnp.float32), 0.1, 1.9)
    w_gate = gaussian(key_of[7], (2 * EXPERTS, D, FF // 2), D ** -0.5, 0.09375, ((0, 32),))
    w_up = gaussian(key_of[8], (2 * EXPERTS, D, FF // 2), D ** -0.5, 0.09375, ((0, 32),))
    w_down = gaussian(key_of[9], (2 * EXPERTS, FF // 2, D), FF ** -0.5, 0.15625, ((0, 32),))
    expert_ids_keys = jax.random.split(jax.random.fold_in(part_keys[10], 1), TOKENS // TOK_DEV)
    expert_ids_turns = jax.random.permutation(jax.random.fold_in(part_keys[10], 3), TOKENS // TOK_DEV)
    expert_ids = jax.vmap(lambda own, number: shared_out(jax.random.fold_in(part_keys[10], 2), own, number, TOK_DEV, EXPERTS, TOP, CAP, 2))(expert_ids_keys, expert_ids_turns).reshape((TOKENS, TOP))
    combine_weights = jnp.clip(jnp.exp(math.log(0.3) - 1.7917595 * jax.random.uniform(part_keys[11], (TOKENS, TOP), jnp.float32) ** block_scale(part_keys[11], (TOKENS, TOP), ((0, 32),), -0.2, 0.2)), 0.05, 0.3)
    return dict(residual=residual, queries=queries, new_kv=new_kv, cache_kv=cache_kv, lengths=lengths, out_weight=out_weight, norm_gain=norm_gain, w_gate=w_gate, w_up=w_up, w_down=w_down, expert_ids=expert_ids, combine_weights=combine_weights)


def attend(queries, new_kv, cache_kv, lengths):
    count_rows = queries.shape[0]
    span = cache_kv.shape[2]
    per_group = H // KVH
    score_scale = 1.0 / math.sqrt(DH)
    query_heads = queries.astype(jnp.float32).reshape(count_rows, KVH, per_group, DH)
    cached_keys = cache_kv[0].astype(jnp.float32).reshape(count_rows, span, KVH, DH)
    cached_values = cache_kv[1].astype(jnp.float32).reshape(count_rows, span, KVH, DH)
    new_key = new_kv[0].astype(jnp.float32).reshape(count_rows, KVH, DH)
    new_value = new_kv[1].astype(jnp.float32).reshape(count_rows, KVH, DH)
    cached_scores = jnp.einsum('tkgd,tckd->tkgc', query_heads, cached_keys) * score_scale
    own_score = jnp.einsum('tkgd,tkd->tkg', query_heads, new_key) * score_scale
    live_mask = (jnp.arange(span, dtype=jnp.int32)[None, :] < lengths[:, None])[:, None, None, :]
    cached_scores = jnp.where(live_mask, cached_scores, -1e+30)
    row_peak = jnp.maximum(lax.optimization_barrier(jnp.max(cached_scores, axis=-1)), own_score)
    cached_exp = jnp.exp(cached_scores - row_peak[..., None])
    own_exp = jnp.exp(own_score - row_peak)
    denominator = lax.optimization_barrier(jnp.sum(cached_exp, axis=-1)) + own_exp
    cached_probs = (cached_exp / denominator[..., None]).astype(jnp.bfloat16)
    own_probs = (own_exp / denominator).astype(jnp.bfloat16)
    attended = jnp.einsum('tkgc,tckd->tkgd', cached_probs.astype(jnp.float32), cached_values)
    attended = attended + own_probs.astype(jnp.float32)[..., None] * new_value[:, :, None, :]
    return attended.reshape(count_rows, H * DH).astype(jnp.bfloat16)

def normalize(hidden_state, norm_gain):
    values = hidden_state.astype(jnp.float32)
    mean_square = lax.optimization_barrier(jnp.mean(values * values, axis=-1, keepdims=True))
    return (values * lax.rsqrt(mean_square + 1e-06) * norm_gain.astype(jnp.float32)).astype(jnp.bfloat16)

def project_blocks(attn_out, out_weight):
    block_width = H * DH // N_DP
    act_blocks = attn_out.reshape(TOKENS, N_DP, block_width).transpose(1, 0, 2)
    weight_blocks = out_weight.reshape(N_DP, block_width, D)

    def add_block(total, pair):
        act_block, weight_block = pair
        partial_sum = jnp.dot(act_block, weight_block, preferred_element_type=jnp.float32).astype(jnp.bfloat16)
        return (total + partial_sum.astype(jnp.float32), None)
    total, _ = lax.scan(add_block, jnp.zeros((TOKENS, D), jnp.float32), (act_blocks, weight_blocks))
    return total

def reference(residual, queries, new_kv, cache_kv, lengths, out_weight, norm_gain, w_gate, w_up, w_down, expert_ids, combine_weights):
    attn_out = attend(queries, new_kv, cache_kv, lengths)
    projected = project_blocks(attn_out, out_weight)
    hidden_state = (residual.astype(jnp.float32) + projected).astype(jnp.bfloat16)
    normed = normalize(hidden_state, norm_gain)
    capacity = min(TOK_DEV, 4 * TOK_DEV * TOP // N_DP)
    limit = N_DP * capacity

    def one_expert(running, expert):
        chosen = expert_ids == expert
        pick_weight = lax.optimization_barrier(jnp.sum(jnp.where(chosen, combine_weights, 0.0), axis=1))
        chosen_any = jnp.any(chosen, axis=1)
        slot_rows = jnp.nonzero(chosen_any, size=limit, fill_value=0)[0].astype(jnp.int32)
        valid = jnp.arange(limit, dtype=jnp.int32) < jnp.sum(chosen_any.astype(jnp.int32))
        picked = normed[slot_rows]
        expert_sum = jnp.zeros((limit, D), jnp.float32)
        for half_index in range(2):
            shard_index = 2 * expert + half_index
            gate_part = jnp.dot(picked, w_gate[shard_index], preferred_element_type=jnp.float32)
            up_part = jnp.dot(picked, w_up[shard_index], preferred_element_type=jnp.float32)
            activated = (jax.nn.silu(gate_part) * up_part).astype(jnp.bfloat16)
            half_out = jnp.dot(activated, w_down[shard_index], preferred_element_type=jnp.float32).astype(jnp.bfloat16)
            expert_sum = expert_sum + half_out.astype(jnp.float32)
        contrib = jnp.where(valid[:, None], pick_weight[slot_rows][:, None] * expert_sum, 0.0)
        return (running.at[slot_rows].add(contrib), None)
    start = jnp.zeros((TOKENS, D), jnp.float32)
    mixture, _ = lax.scan(one_expert, start, jnp.arange(EXPERTS, dtype=jnp.int32))
    return (hidden_state.astype(jnp.float32) + mixture).astype(jnp.bfloat16)
```

```python
import math

import jax
import jax.numpy as jnp
from jax import lax
from jax.sharding import PartitionSpec as P

H = 64
KVH = 4
DH = 128
TOP = 8
F32 = jnp.float32
BF16 = jnp.bfloat16


def attend(queries, new_kv, cache_kv, lengths):
    count_rows = queries.shape[0]
    span = cache_kv.shape[2]
    per_group = H // KVH
    score_scale = 1.0 / math.sqrt(DH)
    query_heads = queries.reshape(count_rows, KVH, per_group, DH)
    cached_keys = cache_kv[0].reshape(count_rows, span, KVH, DH)
    cached_values = cache_kv[1].reshape(count_rows, span, KVH, DH)
    new_key = new_kv[0].reshape(count_rows, KVH, DH)
    new_value = new_kv[1].reshape(count_rows, KVH, DH)
    cached_scores = (
        jnp.einsum("tkgd,tckd->tkgc", query_heads, cached_keys, preferred_element_type=jnp.float32)
        * score_scale
    )
    own_score = (
        jnp.einsum("tkgd,tkd->tkg", query_heads, new_key, preferred_element_type=jnp.float32)
        * score_scale
    )
    live_mask = (jnp.arange(span, dtype=jnp.int32)[None, :] < lengths[:, None])[:, None, None, :]
    cached_scores = jnp.where(live_mask, cached_scores, -1e30)
    row_peak = jnp.maximum(jnp.max(cached_scores, axis=-1), own_score)
    cached_exp = jnp.exp(cached_scores - row_peak[..., None])
    own_exp = jnp.exp(own_score - row_peak)
    denominator = jnp.sum(cached_exp, axis=-1) + own_exp
    cached_probs = (cached_exp / denominator[..., None]).astype(jnp.bfloat16)
    own_probs = (own_exp / denominator).astype(jnp.bfloat16)
    attended = jnp.einsum(
        "tkgc,tckd->tkgd", cached_probs, cached_values, preferred_element_type=jnp.float32
    )
    attended = (
        attended
        + own_probs.astype(jnp.float32)[..., None] * new_value.astype(jnp.float32)[:, :, None, :]
    )
    return attended.reshape(count_rows, H * DH).astype(jnp.bfloat16)


def normalize(hidden_state, norm_gain):
    values = hidden_state.astype(jnp.float32)
    mean_square = jnp.mean(values * values, axis=-1, keepdims=True)
    return (values * lax.rsqrt(mean_square + 1e-06) * norm_gain).astype(jnp.bfloat16)


def step_bits(devices):
    bits = [1 << i for i in range(1, devices.bit_length() - 1)]
    other = bits[1::-1] + bits[2:] if len(bits) > 1 else bits
    return bits, other


def swap_step(step, devices):
    orders = step_bits(devices)
    return [(i, i ^ orders[i & 1][step]) for i in range(devices)]


def reduce_slots(parts, rows, devices):
    steps = devices.bit_length() - 2
    kept = parts
    for step in range(steps):
        half = kept.shape[0] // 2
        came = lax.ppermute(kept[half:].astype(BF16), "dp", swap_step(step, devices))
        kept = kept[:half].astype(F32) + came.astype(F32)
    return kept


def gather_slots(own, devices):
    steps = devices.bit_length() - 2
    for step in reversed(range(steps)):
        own = jnp.concatenate([own, lax.ppermute(own, "dp", swap_step(step, devices))], axis=0)
    return own


def per_device(
    residual,
    queries,
    new_kv,
    cache_kv,
    lengths,
    out_weight,
    norm_gain,
    w_gate,
    w_up,
    w_down,
    expert_ids,
    combine_weights,
):
    rows = residual.shape[0]
    width = residual.shape[1]
    devices = lax.axis_size("dp")
    chips = devices // 2
    block = out_weight.shape[0]
    me = lax.axis_index("dp")
    core = me % 2
    chip = me // 2
    steps = devices.bit_length() - 2
    core_swap = [(i, i ^ 1) for i in range(devices)]
    core_groups = [[2 * i + c for i in range(chips)] for c in range(2)]

    out_other = lax.ppermute(out_weight, "dp", core_swap)
    gate_other = lax.ppermute(w_gate[0], "dp", core_swap)
    up_other = lax.ppermute(w_up[0], "dp", core_swap)
    down_other = lax.ppermute(w_down[0], "dp", core_swap)

    attn_out = attend(queries, new_kv, cache_kv, lengths).reshape(rows, chips, 2, block)
    attn_out = jnp.where(core == 0, attn_out, attn_out[:, :, ::-1]).reshape(rows, chips * 2 * block)
    blocks = lax.all_to_all(
        attn_out, "dp", split_axis=1, concat_axis=0, axis_index_groups=core_groups, tiled=True
    ).reshape(chips, rows, 2 * block)

    orders = step_bits(devices)
    slot = jnp.arange(chips, dtype=jnp.int32)
    offset = jnp.zeros_like(slot)
    for step in range(steps):
        here = jnp.where(core == 0, orders[0][step], orders[1][step]) // 2
        offset = offset + here * ((slot >> (steps - 1 - step)) & 1)
    blocks = jnp.take(blocks, chip ^ offset, axis=0).reshape(chips * rows, 2 * block)

    partial = jnp.dot(blocks[:, :block], out_weight, preferred_element_type=F32) + jnp.dot(
        blocks[:, block:], out_other, preferred_element_type=F32
    )
    projected = reduce_slots(partial.astype(BF16), rows, devices)
    hidden_state = (residual.astype(F32) + projected).astype(BF16)
    normed = normalize(hidden_state, norm_gain)

    picks = expert_ids[:, :, None] == jnp.arange(chips, dtype=jnp.int32)
    mix = jnp.sum(jnp.where(picks, combine_weights[:, :, None], 0.0), axis=1)
    mix_hi = mix.astype(BF16)
    mix_mid = (mix - mix_hi.astype(F32)).astype(BF16)
    mix_low = (mix - mix_hi.astype(F32) - mix_mid.astype(F32)).astype(BF16)
    extra = jnp.concatenate([mix_hi, mix_mid, mix_low], axis=1)
    extra = jnp.pad(extra, ((0, 0), (0, -extra.shape[1] % 128)))
    gathered = gather_slots(jnp.concatenate([normed, extra], axis=1), devices)
    tokens = gathered[:, :width]
    extra = gathered[:, width : width + 3 * chips].reshape(chips * rows, 3, chips).astype(F32)
    mine = jnp.where(jnp.arange(chips) == chip, extra, 0.0)
    weight = jnp.sum(mine, axis=(1, 2))[:, None]

    total = 0.0
    for gate, up, down in ((w_gate[0], w_up[0], w_down[0]), (gate_other, up_other, down_other)):
        gate_part = jnp.dot(tokens, gate, preferred_element_type=F32)
        up_part = jnp.dot(tokens, up, preferred_element_type=F32)
        activated = (jax.nn.silu(gate_part) * up_part).astype(BF16)
        total = total + jnp.dot(activated, down, preferred_element_type=F32)
    mixture = reduce_slots((total * weight).astype(BF16), rows, devices)
    return (hidden_state.astype(F32) + mixture).astype(BF16)


def solution(mesh):
    placed = (
        P(("groups", "dp"), None),
        P(("groups", "dp"), None),
        P(None, ("groups", "dp"), None),
        P(None, ("groups", "dp"), None, None),
        P(("groups", "dp")),
        P("dp", None),
        P(),
        P("dp", None, None),
        P("dp", None, None),
        P("dp", None, None),
        P(("groups", "dp"), None),
        P(("groups", "dp"), None),
    )
    return jax.shard_map(
        per_device, mesh=mesh, in_specs=placed, out_specs=P(("groups", "dp"), None), check_vma=False
    )
```

```python
import math

import jax
import jax.numpy as jnp
from jax import lax
from jax.experimental import pallas as pl
from jax.experimental.pallas import tpu as pltpu
from jax.sharding import PartitionSpec as P

H = 64
KVH = 4
DH = 128
TOP = 8
F32 = jnp.float32
BF16 = jnp.bfloat16


def attend_kernel(core_ref, lengths_ref, q_ref, new_ref, cache_ref, out_ref, q_rows, out_rows):
    rows = q_ref.shape[0]
    heads = q_ref.shape[1] // DH
    per_group = heads // KVH
    count = cache_ref.shape[1]
    span = cache_ref.shape[2]
    step = pl.program_id(0)
    scale = 1.0 / math.sqrt(DH)

    @pl.when(step == 0)
    def _():
        for h in range(heads):
            q_rows[h * rows : (h + 1) * rows, :] = q_ref[:, h * DH : (h + 1) * DH].astype(F32)

    position = lax.broadcasted_iota(jnp.int32, (heads, span), 1)
    for i in range(count):
        t = step * count + i
        query = q_rows[pl.ds(t, heads, stride=rows), :]
        query16 = query.astype(BF16)
        new_key = new_ref[0, pl.ds(t, 1), :]
        new_value = new_ref[1, pl.ds(t, 1), :]
        scores, own = [], []
        for g in range(KVH):
            part = slice(g * per_group, (g + 1) * per_group)
            lanes = slice(g * DH, (g + 1) * DH)
            scores.append(
                lax.dot_general(
                    query16[part],
                    cache_ref[0, i, :, lanes],
                    (((1,), (1,)), ((), ())),
                    preferred_element_type=F32,
                )
            )
            own.append(jnp.sum(query[part] * new_key[:, lanes], axis=1, keepdims=True))
        scores = jnp.concatenate(scores, axis=0) * scale
        own = jnp.concatenate(own, axis=0) * scale
        scores = jnp.where(position < lengths_ref[t], scores, -1e30)
        peak = jnp.maximum(jnp.max(scores, axis=1, keepdims=True), own)
        cached_exp = jnp.exp(scores - peak)
        own_exp = jnp.exp(own - peak)
        denominator = jnp.sum(cached_exp, axis=1, keepdims=True) + own_exp
        probs = (cached_exp / denominator).astype(BF16)
        own_probs = (own_exp / denominator).astype(BF16).astype(F32)
        for g in range(KVH):
            part = slice(g * per_group, (g + 1) * per_group)
            lanes = slice(g * DH, (g + 1) * DH)
            value = jnp.dot(probs[part], cache_ref[1, i, :, lanes], preferred_element_type=F32)
            value = value + own_probs[part] * new_value[:, lanes]
            out_rows[pl.ds(g * per_group * rows + t, per_group, stride=rows), :] = value

    chips = out_ref.shape[0]
    per_chip = heads // chips
    for side in range(2):

        @pl.when((step == pl.num_programs(0) - 1) & (core_ref[0] == side))
        def _():
            for e in range(chips):
                for i in range(per_chip):
                    h = e * per_chip + (i + side * (per_chip // 2)) % per_chip
                    out_ref[e, :, i * DH : (i + 1) * DH] = out_rows[h * rows : (h + 1) * rows, :].astype(BF16)


def attend(core, queries, new_kv, cache_kv, lengths, chips):
    rows, features = queries.shape
    span, width = cache_kv.shape[2:]
    count = 4 if rows % 4 == 0 else 1
    whole = lambda shape: pl.BlockSpec(shape, lambda s, *_: (0,) * len(shape))
    return pl.pallas_call(
        attend_kernel,
        out_shape=jax.ShapeDtypeStruct((chips, rows, features // chips), BF16),
        grid_spec=pltpu.PrefetchScalarGridSpec(
            num_scalar_prefetch=2,
            grid=(rows // count,),
            in_specs=[
                whole((rows, features)),
                whole((2, rows, width)),
                pl.BlockSpec((2, count, span, width), lambda s, *_: (0, s, 0, 0)),
            ],
            out_specs=whole((chips, rows, features // chips)),
            scratch_shapes=[
                pltpu.VMEM((features // DH * rows, DH), F32),
                pltpu.VMEM((features // DH * rows, DH), F32),
            ],
        ),
        compiler_params=pltpu.CompilerParams(vmem_limit_bytes=24 << 20),
        cost_estimate=pl.CostEstimate(flops=4 * rows * features * span, bytes_accessed=2 * cache_kv.size, transcendentals=rows * features),
    )(core, lengths, queries, new_kv.astype(F32), cache_kv)


def project_kernel(index_ref, blocks_ref, own_ref, other_ref, keep_ref, send_ref, ordered):
    chips, rows, features = blocks_ref.shape
    half = features // 2

    @pl.when(pl.program_id(0) == 0)
    def _():
        for k in range(chips):
            ordered[k * rows : (k + 1) * rows, :] = blocks_ref[index_ref[k]]

    total = jnp.dot(ordered[:, :half], own_ref[...], preferred_element_type=F32)
    total = total + jnp.dot(ordered[:, half:], other_ref[...], preferred_element_type=F32)
    cut = keep_ref.shape[0]
    keep_ref[...] = total[:cut].astype(BF16)
    send_ref[...] = total[cut:].astype(BF16)


def project(index, blocks, own, other):
    chips, rows, features = blocks.shape
    depth, width = own.shape
    tile = 512
    weights = pl.BlockSpec((depth, tile), lambda s, *_: (0, s))
    result = pl.BlockSpec((chips * rows // 2, tile), lambda s, *_: (0, s))
    return pl.pallas_call(
        project_kernel,
        out_shape=[jax.ShapeDtypeStruct((chips * rows // 2, width), BF16)] * 2,
        grid_spec=pltpu.PrefetchScalarGridSpec(
            num_scalar_prefetch=1,
            grid=(width // tile,),
            in_specs=[pl.BlockSpec(blocks.shape, lambda s, *_: (0, 0, 0)), weights, weights],
            out_specs=[result, result],
            scratch_shapes=[pltpu.VMEM((chips * rows, features), BF16)],
        ),
        compiler_params=pltpu.CompilerParams(vmem_limit_bytes=24 << 20),
        cost_estimate=pl.CostEstimate(flops=2 * blocks.size * width, bytes_accessed=4 * own.size, transcendentals=0),
    )(index, blocks, own, other)


F_TILE = 256
N_TILE = 512


def expert_kernel(
    chip_ref, low_ref, high_ref, gate0, gate1, up0, up1, down0, down1, keep_ref, send_ref,
    tokens, gates, ups, downs, active, gate_sem, up_sem, down_sem,
):
    half, width = keep_ref.shape
    hidden = gate0.shape[1]
    per_half = hidden // F_TILE
    copies = []
    for j, (gate, up) in enumerate(((gate0, up0), (gate1, up1))):
        for i in range(per_half):
            t = j * per_half + i
            lanes = pl.ds(i * F_TILE, F_TILE)
            copies.append(pltpu.make_async_copy(gate.at[:, lanes], gates.at[t], gate_sem.at[t]))
            copies.append(pltpu.make_async_copy(up.at[:, lanes], ups.at[t], up_sem.at[t]))
    n_tiles = width // N_TILE
    for n in range(n_tiles):
        for j, down in enumerate((down0, down1)):
            copies.append(
                pltpu.make_async_copy(
                    down.at[:, pl.ds(n * N_TILE, N_TILE)],
                    downs.at[n, pl.ds(j * hidden, hidden), :],
                    down_sem.at[n, j],
                )
            )
    for copy in copies:
        copy.start()
    tokens[:half, :] = low_ref[:, :width]
    tokens[half:, :] = high_ref[:, :width]

    for t in range(2 * per_half):
        copies[2 * t].wait()
        gate_part = jnp.dot(tokens[...], gates[t], preferred_element_type=F32)
        copies[2 * t + 1].wait()
        up_part = jnp.dot(tokens[...], ups[t], preferred_element_type=F32)
        lanes = slice(t * F_TILE, (t + 1) * F_TILE)
        active[:, lanes] = (gate_part / (1.0 + jnp.exp(-gate_part)) * up_part).astype(BF16)

    chips = chip_ref[1]
    lane = lax.broadcasted_iota(jnp.int32, (half, low_ref.shape[1] - width), 1)
    first = chip_ref[0]
    mine = (lane == first) | (lane == first + chips) | (lane == first + 2 * chips)
    weights = [
        jnp.sum(jnp.where(mine, ref[:, width:].astype(F32), 0.0), axis=1, keepdims=True)
        for ref in (low_ref, high_ref)
    ]
    for n in range(n_tiles):
        copies[4 * per_half + 2 * n].wait()
        copies[4 * per_half + 2 * n + 1].wait()
        total = jnp.dot(active[...], downs[n], preferred_element_type=F32)
        lanes = slice(n * N_TILE, (n + 1) * N_TILE)
        keep_ref[:, lanes] = (total[:half] * weights[0]).astype(BF16)
        send_ref[:, lanes] = (total[half:] * weights[1]).astype(BF16)


def experts(chip, low, high, gates, ups, downs):
    half = low.shape[0]
    width, hidden = gates[0].shape
    tiles = 2 * hidden // F_TILE
    blocks = width // N_TILE
    any_space = pl.BlockSpec(memory_space=pl.ANY)
    vmem = pl.BlockSpec(memory_space=pltpu.VMEM)
    return pl.pallas_call(
        expert_kernel,
        out_shape=[jax.ShapeDtypeStruct((half, width), BF16)] * 2,
        in_specs=[pl.BlockSpec(memory_space=pltpu.SMEM), vmem, vmem] + [any_space] * 6,
        out_specs=[vmem, vmem],
        scratch_shapes=[
            pltpu.VMEM((2 * half, width), BF16),
            pltpu.VMEM((tiles, width, F_TILE), BF16),
            pltpu.VMEM((tiles, width, F_TILE), BF16),
            pltpu.VMEM((blocks, 2 * hidden, N_TILE), BF16),
            pltpu.VMEM((2 * half, 2 * hidden), BF16),
            pltpu.SemaphoreType.DMA((tiles,)),
            pltpu.SemaphoreType.DMA((tiles,)),
            pltpu.SemaphoreType.DMA((blocks, 2)),
        ],
        compiler_params=pltpu.CompilerParams(vmem_limit_bytes=56 << 20),
        cost_estimate=pl.CostEstimate(flops=24 * half * width * hidden, bytes_accessed=12 * width * hidden, transcendentals=4 * half * hidden),
    )(chip, low, high, *gates, *ups, *downs)


def normalize(hidden_state, norm_gain):
    values = hidden_state.astype(jnp.float32)
    mean_square = jnp.mean(values * values, axis=-1, keepdims=True)
    return (values * lax.rsqrt(mean_square + 1e-06) * norm_gain).astype(jnp.bfloat16)


def step_bits(devices):
    bits = [1 << i for i in range(1, devices.bit_length() - 1)]
    other = bits[1::-1] + bits[2:] if len(bits) > 1 else bits
    return bits, other


def swap_step(step, devices):
    orders = step_bits(devices)
    return [(i, i ^ orders[i & 1][step]) for i in range(devices)]


def reduce_slots(kept, sent, devices):
    steps = devices.bit_length() - 2
    for step in range(steps):
        came = lax.ppermute(sent, "dp", swap_step(step, devices))
        kept = kept.astype(F32) + came.astype(F32)
        half = kept.shape[0] // 2
        if step < steps - 1:
            sent = kept[half:].astype(BF16)
            kept = kept[:half]
    return kept


def gather_slots(own, devices):
    steps = devices.bit_length() - 2
    for step in reversed(range(steps)):
        came = lax.ppermute(own, "dp", swap_step(step, devices))
        if step == 0:
            return own, came
        own = jnp.concatenate([own, came], axis=0)


def per_device(
    residual,
    queries,
    new_kv,
    cache_kv,
    lengths,
    out_weight,
    norm_gain,
    w_gate,
    w_up,
    w_down,
    expert_ids,
    combine_weights,
):
    rows = residual.shape[0]
    width = residual.shape[1]
    devices = lax.axis_size("dp")
    chips = devices // 2
    me = lax.axis_index("dp")
    core = me % 2
    chip = me // 2
    steps = devices.bit_length() - 2
    core_swap = [(i, i ^ 1) for i in range(devices)]
    core_groups = [[2 * i + c for i in range(chips)] for c in range(2)]

    out_other = lax.ppermute(out_weight, "dp", core_swap)
    gate_other = lax.ppermute(w_gate[0], "dp", core_swap)
    up_other = lax.ppermute(w_up[0], "dp", core_swap)
    down_other = lax.ppermute(w_down[0], "dp", core_swap)

    attn_out = attend(core[None], queries, new_kv, cache_kv, lengths, chips)
    blocks = lax.all_to_all(
        attn_out, "dp", split_axis=0, concat_axis=0, axis_index_groups=core_groups, tiled=True
    )

    orders = step_bits(devices)
    slot = jnp.arange(chips, dtype=jnp.int32)
    offset = jnp.zeros_like(slot)
    for step in range(steps):
        here = jnp.where(core == 0, orders[0][step], orders[1][step]) // 2
        offset = offset + here * ((slot >> (steps - 1 - step)) & 1)
    kept, sent = project(chip ^ offset, blocks, out_weight, out_other)
    projected = reduce_slots(kept, sent, devices)
    hidden_state = (residual.astype(F32) + projected).astype(BF16)
    normed = normalize(hidden_state, norm_gain)

    picks = expert_ids[:, :, None] == jnp.arange(chips, dtype=jnp.int32)
    mix = jnp.sum(jnp.where(picks, combine_weights[:, :, None], 0.0), axis=1)
    mix_hi = mix.astype(BF16)
    mix_mid = (mix - mix_hi.astype(F32)).astype(BF16)
    mix_low = (mix - mix_hi.astype(F32) - mix_mid.astype(F32)).astype(BF16)
    extra = jnp.concatenate([mix_hi, mix_mid, mix_low], axis=1)
    extra = jnp.pad(extra, ((0, 0), (0, -extra.shape[1] % 128)))
    low, high = gather_slots(jnp.concatenate([normed, extra], axis=1), devices)
    place = jnp.stack([chip, jnp.int32(chips)])
    kept, sent = experts(
        place, low, high, (w_gate[0], gate_other), (w_up[0], up_other), (w_down[0], down_other)
    )
    mixture = reduce_slots(kept, sent, devices)
    return (hidden_state.astype(F32) + mixture).astype(BF16)


def solution(mesh):
    placed = (
        P(("groups", "dp"), None),
        P(("groups", "dp"), None),
        P(None, ("groups", "dp"), None),
        P(None, ("groups", "dp"), None, None),
        P(("groups", "dp")),
        P("dp", None),
        P(),
        P("dp", None, None),
        P("dp", None, None),
        P("dp", None, None),
        P(("groups", "dp"), None),
        P(("groups", "dp"), None),
    )
    return jax.shard_map(
        per_device, mesh=mesh, in_specs=placed, out_specs=P(("groups", "dp"), None), check_vma=False
    )
```

```python
import math

import jax
import jax.numpy as jnp
from jax import lax
from jax.experimental import pallas as pl
from jax.experimental.pallas import tpu as pltpu
from jax.sharding import PartitionSpec as P

H = 64
KVH = 4
DH = 128
TOP = 8
F32 = jnp.float32
BF16 = jnp.bfloat16


CHUNKS = 2


def attend_kernel(core_ref, lengths_ref, q_ref, new_ref, cache_ref, out_ref, q_rows, out_rows, new_rows):
    rows = q_ref.shape[0]
    heads = q_ref.shape[1] // DH
    per_group = heads // KVH
    count = cache_ref.shape[1]
    span, width = cache_ref.shape[2:]
    step = pl.program_id(0)
    scale = 1.0 / math.sqrt(DH)

    @pl.when(step == 0)
    def _():
        new_rows[...] = new_ref[...].astype(F32)
        for h in range(heads):
            q_rows[h * rows : (h + 1) * rows, :] = q_ref[:, h * DH : (h + 1) * DH].astype(F32)

    position = lax.broadcasted_iota(jnp.int32, (heads, span), 1)
    row_group = lax.broadcasted_iota(jnp.int32, (heads, width), 0) // per_group
    lane_group = lax.broadcasted_iota(jnp.int32, (heads, width), 1) // DH
    own_lanes = row_group == lane_group
    for i in range(count):
        t = step * count + i
        query = q_rows[pl.ds(t, heads, stride=rows), :]
        new_key = new_rows[0, pl.ds(t, 1), :]
        new_value = new_rows[1, pl.ds(t, 1), :]
        spread = jnp.where(own_lanes, jnp.concatenate([query] * KVH, axis=1), 0.0)
        scores = lax.dot_general(
            spread.astype(BF16), cache_ref[0, i], (((1,), (1,)), ((), ())), preferred_element_type=F32
        )
        own = jnp.sum(spread * new_key, axis=1, keepdims=True) * scale
        scores = jnp.where(position < lengths_ref[t], scores * scale, -1e30)
        peak = jnp.maximum(jnp.max(scores, axis=1, keepdims=True), own)
        cached_exp = jnp.exp(scores - peak)
        own_exp = jnp.exp(own - peak)
        denominator = jnp.sum(cached_exp, axis=1, keepdims=True) + own_exp
        probs = (cached_exp / denominator).astype(BF16)
        own_probs = (own_exp / denominator).astype(BF16).astype(F32)
        values = jnp.dot(probs, cache_ref[1, i], preferred_element_type=F32)
        for g in range(KVH):
            part = slice(g * per_group, (g + 1) * per_group)
            lanes = slice(g * DH, (g + 1) * DH)
            value = values[part, lanes] + own_probs[part] * new_value[:, lanes]
            out_rows[pl.ds(g * per_group * rows + t, per_group, stride=rows), :] = value

    chips = out_ref.shape[0]
    per_chip = heads // chips
    for side in range(2):

        @pl.when((step == pl.num_programs(0) - 1) & (core_ref[0] == side))
        def _():
            for e in range(chips):
                for i in range(per_chip):
                    h = e * per_chip + (i + side * (per_chip // 2)) % per_chip
                    out_ref[e, :, i * DH : (i + 1) * DH] = out_rows[h * rows : (h + 1) * rows, :].astype(BF16)


def attend(core, queries, new_kv, cache_kv, lengths, chips):
    rows, features = queries.shape
    span, width = cache_kv.shape[2:]
    count = 4 if rows % 4 == 0 else 1
    whole = lambda shape: pl.BlockSpec(shape, lambda s, *_: (0,) * len(shape))
    return pl.pallas_call(
        attend_kernel,
        out_shape=jax.ShapeDtypeStruct((chips, rows, features // chips), BF16),
        grid_spec=pltpu.PrefetchScalarGridSpec(
            num_scalar_prefetch=2,
            grid=(rows // count,),
            in_specs=[
                whole((rows, features)),
                whole((2, rows, width)),
                pl.BlockSpec((2, count, span, width), lambda s, *_: (0, s, 0, 0)),
            ],
            out_specs=whole((chips, rows, features // chips)),
            scratch_shapes=[
                pltpu.VMEM((features // DH * rows, DH), F32),
                pltpu.VMEM((features // DH * rows, DH), F32),
                pltpu.VMEM((2, rows, width), F32),
            ],
        ),
        compiler_params=pltpu.CompilerParams(vmem_limit_bytes=58 << 20),
        cost_estimate=pl.CostEstimate(flops=4 * rows * features * span, bytes_accessed=2 * cache_kv.size, transcendentals=rows * features),
    )(core, lengths, queries, new_kv, cache_kv)


P_TILE = 512


def project_kernel(index_ref, blocks_ref, own_ref, other_ref, *rest):
    results, ordered = rest[:-1], rest[-1]
    chips, rows, features = blocks_ref.shape
    half = features // 2
    cut = results[0].shape[0]
    chunk = results[0].shape[1]
    for k in range(chips):
        ordered[k * rows : (k + 1) * rows, :] = blocks_ref[index_ref[k]]
    for n in range(own_ref.shape[1] // P_TILE):
        lanes = slice(n * P_TILE, (n + 1) * P_TILE)
        total = jnp.dot(ordered[:, :half], own_ref[:, lanes], preferred_element_type=F32)
        total = total + jnp.dot(ordered[:, half:], other_ref[:, lanes], preferred_element_type=F32)
        c, at = divmod(n * P_TILE, chunk)
        lanes = slice(at, at + P_TILE)
        results[2 * c][:, lanes] = total[:cut].astype(BF16)
        results[2 * c + 1][:, lanes] = total[cut:].astype(BF16)


def project(index, blocks, own, other):
    chips, rows, features = blocks.shape
    width = own.shape[1]
    vmem = pl.BlockSpec(memory_space=pltpu.VMEM)
    return pl.pallas_call(
        project_kernel,
        out_shape=[jax.ShapeDtypeStruct((chips * rows // 2, width // CHUNKS), BF16)] * (2 * CHUNKS),
        in_specs=[pl.BlockSpec(memory_space=pltpu.SMEM), vmem, vmem, vmem],
        out_specs=[vmem] * (2 * CHUNKS),
        scratch_shapes=[pltpu.VMEM((chips * rows, features), BF16)],
        compiler_params=pltpu.CompilerParams(vmem_limit_bytes=12 << 20),
        cost_estimate=pl.CostEstimate(flops=2 * blocks.size * width, bytes_accessed=4 * own.size, transcendentals=0),
    )(index, blocks, own, other)


F_TILE = 256
N_TILE = 512


def expert_kernel(chip_ref, *refs):
    pieces, refs = refs[: 2 * CHUNKS], refs[2 * CHUNKS :]
    (gate0, gate1, up0, up1, down0, down1), refs = refs[:6], refs[6:]
    results, (tokens, active) = refs[: 2 * CHUNKS], refs[2 * CHUNKS :]
    half, chunk = results[0].shape
    hidden = gate0.shape[1]
    per_half = hidden // F_TILE
    for c in range(CHUNKS):
        for side in range(2):
            tokens[side * half : (side + 1) * half, c * chunk : (c + 1) * chunk] = pieces[2 * c + side][:, :chunk]

    for j, (gate, up) in enumerate(((gate0, up0), (gate1, up1))):
        for i in range(per_half):
            lanes = slice(i * F_TILE, (i + 1) * F_TILE)
            gate_part = jnp.dot(tokens[...], gate[:, lanes], preferred_element_type=F32)
            up_part = jnp.dot(tokens[...], up[:, lanes], preferred_element_type=F32)
            at = j * hidden + i * F_TILE
            active[:, at : at + F_TILE] = (gate_part / (1.0 + jnp.exp(-gate_part)) * up_part).astype(BF16)

    first, chips = chip_ref[0], chip_ref[1]
    lane = lax.broadcasted_iota(jnp.int32, (half, pieces[0].shape[1] - chunk), 1)
    mine = (lane == first) | (lane == first + chips) | (lane == first + 2 * chips)
    weights = [
        jnp.sum(jnp.where(mine, ref[:, chunk:].astype(F32), 0.0), axis=1, keepdims=True) for ref in pieces[:2]
    ]
    for n in range(CHUNKS * chunk // N_TILE):
        lanes = slice(n * N_TILE, (n + 1) * N_TILE)
        total = jnp.dot(active[:, :hidden], down0[:, lanes], preferred_element_type=F32)
        total = total + jnp.dot(active[:, hidden:], down1[:, lanes], preferred_element_type=F32)
        c, at = divmod(n * N_TILE, chunk)
        lanes = slice(at, at + N_TILE)
        results[2 * c][:, lanes] = (total[:half] * weights[0]).astype(BF16)
        results[2 * c + 1][:, lanes] = (total[half:] * weights[1]).astype(BF16)


def experts(chip, pieces, gates, ups, downs):
    half = pieces[0].shape[0]
    width, hidden = gates[0].shape
    vmem = pl.BlockSpec(memory_space=pltpu.VMEM)
    return pl.pallas_call(
        expert_kernel,
        out_shape=[jax.ShapeDtypeStruct((half, width // CHUNKS), BF16)] * (2 * CHUNKS),
        in_specs=[pl.BlockSpec(memory_space=pltpu.SMEM)] + [vmem] * (2 * CHUNKS + 6),
        out_specs=[vmem] * (2 * CHUNKS),
        scratch_shapes=[pltpu.VMEM((2 * half, width), BF16), pltpu.VMEM((2 * half, 2 * hidden), BF16)],
        compiler_params=pltpu.CompilerParams(vmem_limit_bytes=28 << 20),
        cost_estimate=pl.CostEstimate(flops=24 * half * width * hidden, bytes_accessed=12 * width * hidden, transcendentals=4 * half * hidden),
    )(chip, *pieces, *gates, *ups, *downs)


def normalize(hidden_state, norm_gain):
    values = [part.astype(F32) for part in hidden_state]
    square = sum(jnp.sum(part * part, axis=-1, keepdims=True) for part in values)
    scale = lax.rsqrt(square / norm_gain.size + 1e-06)
    gains = jnp.split(norm_gain, CHUNKS)
    return [(part * scale * gain).astype(BF16) for part, gain in zip(values, gains)]


def step_bits(devices):
    bits = [1 << i for i in range(1, devices.bit_length() - 1)]
    other = bits[1::-1] + bits[2:] if len(bits) > 1 else bits
    return bits, other


def swap_step(step, devices):
    orders = step_bits(devices)
    return [(i, i ^ orders[i & 1][step]) for i in range(devices)]


def reduce_slots(pieces, devices):
    steps = devices.bit_length() - 2
    kept, sent = list(pieces[::2]), list(pieces[1::2])
    for step in range(steps):
        for c in range(CHUNKS):
            came = lax.ppermute(sent[c], "dp", swap_step(step, devices))
            kept[c] = kept[c].astype(F32) + came.astype(F32)
            half = kept[c].shape[0] // 2
            if step < steps - 1:
                sent[c] = kept[c][half:].astype(BF16)
                kept[c] = kept[c][:half]
    return kept


def gather_slots(own, devices):
    own = list(own)
    steps = devices.bit_length() - 2
    pieces = []
    for step in reversed(range(steps)):
        for c in range(CHUNKS):
            came = lax.ppermute(own[c], "dp", swap_step(step, devices))
            if step == 0:
                pieces += [own[c], came]
            else:
                own[c] = jnp.concatenate([own[c], came], axis=0)
    return pieces


def per_device(
    residual,
    queries,
    new_kv,
    cache_kv,
    lengths,
    out_weight,
    norm_gain,
    w_gate,
    w_up,
    w_down,
    expert_ids,
    combine_weights,
):
    rows = residual.shape[0]
    devices = lax.axis_size("dp")
    chips = devices // 2
    me = lax.axis_index("dp")
    core = me % 2
    chip = me // 2
    steps = devices.bit_length() - 2
    core_swap = [(i, i ^ 1) for i in range(devices)]
    core_groups = [[2 * i + c for i in range(chips)] for c in range(2)]

    out_other = lax.ppermute(out_weight, "dp", core_swap)
    gate_other = lax.ppermute(w_gate[0], "dp", core_swap)
    up_other = lax.ppermute(w_up[0], "dp", core_swap)
    down_other = lax.ppermute(w_down[0], "dp", core_swap)

    attn_out = attend(core[None], queries, new_kv, cache_kv, lengths, chips)
    blocks = lax.all_to_all(
        attn_out, "dp", split_axis=0, concat_axis=0, axis_index_groups=core_groups, tiled=True
    )

    orders = step_bits(devices)
    slot = jnp.arange(chips, dtype=jnp.int32)
    offset = jnp.zeros_like(slot)
    for step in range(steps):
        here = jnp.where(core == 0, orders[0][step], orders[1][step]) // 2
        offset = offset + here * ((slot >> (steps - 1 - step)) & 1)
    projected = reduce_slots(project(chip ^ offset, blocks, out_weight, out_other), devices)
    hidden_state = [
        (part.astype(F32) + add).astype(BF16) for part, add in zip(jnp.split(residual, CHUNKS, axis=1), projected)
    ]
    normed = normalize(hidden_state, norm_gain)

    picks = expert_ids[:, :, None] == jnp.arange(chips, dtype=jnp.int32)
    mix = jnp.sum(jnp.where(picks, combine_weights[:, :, None], 0.0), axis=1)
    mix_hi = mix.astype(BF16)
    mix_mid = (mix - mix_hi.astype(F32)).astype(BF16)
    mix_low = (mix - mix_hi.astype(F32) - mix_mid.astype(F32)).astype(BF16)
    extra = jnp.concatenate([mix_hi, mix_mid, mix_low], axis=1)
    extra = jnp.pad(extra, ((0, 0), (0, -extra.shape[1] % 128)))
    normed[0] = jnp.concatenate([normed[0], extra], axis=1)
    pieces = gather_slots(normed, devices)
    place = jnp.stack([chip, jnp.int32(chips)])
    outs = experts(place, pieces, (w_gate[0], gate_other), (w_up[0], up_other), (w_down[0], down_other))
    mixture = reduce_slots(outs, devices)
    return jnp.concatenate(
        [(part.astype(F32) + add).astype(BF16) for part, add in zip(hidden_state, mixture)], axis=1
    )


def solution(mesh):
    placed = (
        P(("groups", "dp"), None),
        P(("groups", "dp"), None),
        P(None, ("groups", "dp"), None),
        P(None, ("groups", "dp"), None, None),
        P(("groups", "dp")),
        P("dp", None),
        P(),
        P("dp", None, None),
        P("dp", None, None),
        P("dp", None, None),
        P(("groups", "dp"), None),
        P(("groups", "dp"), None),
    )
    return jax.shard_map(
        per_device, mesh=mesh, in_specs=placed, out_specs=P(("groups", "dp"), None), check_vma=False
    )
```

```python
import math

import jax
import jax.numpy as jnp
from jax import lax
from jax.experimental import pallas as pl
from jax.experimental.pallas import tpu as pltpu
from jax.sharding import PartitionSpec as P

H = 64
KVH = 4
DH = 128
TOP = 8
F32 = jnp.float32
BF16 = jnp.bfloat16


CHUNKS = 2


def attend_kernel(core_ref, lengths_ref, q_ref, new_ref, cache_ref, out_ref, q_rows, out_rows, new_rows):
    rows = q_ref.shape[0]
    heads = q_ref.shape[1] // DH
    per_group = heads // KVH
    count = cache_ref.shape[1]
    span, width = cache_ref.shape[2:]
    step = pl.program_id(0)
    scale = 1.0 / math.sqrt(DH)

    @pl.when(step == 0)
    def _():
        new_rows[...] = new_ref[...].astype(F32)
        for h in range(heads):
            q_rows[h * rows : (h + 1) * rows, :] = q_ref[:, h * DH : (h + 1) * DH].astype(F32)

    position = lax.broadcasted_iota(jnp.int32, (heads, span), 1)
    row_group = lax.broadcasted_iota(jnp.int32, (heads, width), 0) // per_group
    lane_group = lax.broadcasted_iota(jnp.int32, (heads, width), 1) // DH
    own_lanes = row_group == lane_group
    for i in range(count):
        t = step * count + i
        query = q_rows[pl.ds(t, heads, stride=rows), :]
        new_key = new_rows[0, pl.ds(t, 1), :]
        new_value = new_rows[1, pl.ds(t, 1), :]
        spread = jnp.where(own_lanes, jnp.concatenate([query] * KVH, axis=1), 0.0)
        scores = lax.dot_general(
            spread.astype(BF16), cache_ref[0, i], (((1,), (1,)), ((), ())), preferred_element_type=F32
        )
        own = jnp.sum(spread * new_key, axis=1, keepdims=True) * scale
        scores = jnp.where(position < lengths_ref[t], scores * scale, -1e30)
        peak = jnp.maximum(jnp.max(scores, axis=1, keepdims=True), own)
        cached_exp = jnp.exp(scores - peak)
        own_exp = jnp.exp(own - peak)
        denominator = jnp.sum(cached_exp, axis=1, keepdims=True) + own_exp
        probs = (cached_exp / denominator).astype(BF16)
        own_probs = (own_exp / denominator).astype(BF16).astype(F32)
        values = jnp.dot(probs, cache_ref[1, i], preferred_element_type=F32)
        for g in range(KVH):
            part = slice(g * per_group, (g + 1) * per_group)
            lanes = slice(g * DH, (g + 1) * DH)
            value = values[part, lanes] + own_probs[part] * new_value[:, lanes]
            out_rows[pl.ds(g * per_group * rows + t, per_group, stride=rows), :] = value

    chips = out_ref.shape[0]
    per_chip = heads // chips
    for side in range(2):

        @pl.when((step == pl.num_programs(0) - 1) & (core_ref[0] == side))
        def _():
            for e in range(chips):
                for i in range(per_chip):
                    h = e * per_chip + (i + side * (per_chip // 2)) % per_chip
                    out_ref[e, :, i * DH : (i + 1) * DH] = out_rows[h * rows : (h + 1) * rows, :].astype(BF16)


def attend(core, queries, new_kv, cache_kv, lengths, chips):
    rows, features = queries.shape
    span, width = cache_kv.shape[2:]
    count = 4 if rows % 4 == 0 else 1
    whole = lambda shape: pl.BlockSpec(shape, lambda s, *_: (0,) * len(shape))
    return pl.pallas_call(
        attend_kernel,
        out_shape=jax.ShapeDtypeStruct((chips, rows, features // chips), BF16),
        grid_spec=pltpu.PrefetchScalarGridSpec(
            num_scalar_prefetch=2,
            grid=(rows // count,),
            in_specs=[
                whole((rows, features)),
                whole((2, rows, width)),
                pl.BlockSpec((2, count, span, width), lambda s, *_: (0, s, 0, 0)),
            ],
            out_specs=whole((chips, rows, features // chips)),
            scratch_shapes=[
                pltpu.VMEM((features // DH * rows, DH), F32),
                pltpu.VMEM((features // DH * rows, DH), F32),
                pltpu.VMEM((2, rows, width), F32),
            ],
        ),
        compiler_params=pltpu.CompilerParams(vmem_limit_bytes=58 << 20),
        cost_estimate=pl.CostEstimate(flops=4 * rows * features * span, bytes_accessed=2 * cache_kv.size, transcendentals=rows * features),
    )(core, lengths, queries, new_kv, cache_kv)


P_TILE = 512


def quarters(chunk, half):
    size = half // 2
    order = (0, 2, 1, 3) if chunk % 2 else (0, 1, 2, 3)
    for place, quarter in enumerate(order):
        at = place % 2 * size
        yield place // 2, slice(at, at + size), slice(quarter * size, (quarter + 1) * size)


def project_kernel(index_ref, blocks_ref, own_ref, other_ref, *rest):
    results, ordered = rest[:-1], rest[-1]
    chips, rows, features = blocks_ref.shape
    half = features // 2
    cut = results[0].shape[0]
    chunk = results[0].shape[1]
    for k in range(chips):
        ordered[k * rows : (k + 1) * rows, :] = blocks_ref[index_ref[k]]
    for n in range(own_ref.shape[1] // P_TILE):
        lanes = slice(n * P_TILE, (n + 1) * P_TILE)
        total = jnp.dot(ordered[:, :half], own_ref[:, lanes], preferred_element_type=F32)
        total = total + jnp.dot(ordered[:, half:], other_ref[:, lanes], preferred_element_type=F32)
        c, at = divmod(n * P_TILE, chunk)
        for to, here, where in quarters(c, cut):
            results[2 * c + to][here, at : at + P_TILE] = total[where].astype(BF16)


def project(index, blocks, own, other):
    chips, rows, features = blocks.shape
    width = own.shape[1]
    vmem = pl.BlockSpec(memory_space=pltpu.VMEM)
    return pl.pallas_call(
        project_kernel,
        out_shape=[jax.ShapeDtypeStruct((chips * rows // 2, width // CHUNKS), BF16)] * (2 * CHUNKS),
        in_specs=[pl.BlockSpec(memory_space=pltpu.SMEM), vmem, vmem, vmem],
        out_specs=[vmem] * (2 * CHUNKS),
        scratch_shapes=[pltpu.VMEM((chips * rows, features), BF16)],
        compiler_params=pltpu.CompilerParams(vmem_limit_bytes=12 << 20),
        cost_estimate=pl.CostEstimate(flops=2 * blocks.size * width, bytes_accessed=4 * own.size, transcendentals=0),
    )(index, blocks, own, other)


F_TILE = 256
N_TILE = 512


def expert_kernel(chip_ref, *refs):
    pieces, refs = refs[: 2 * CHUNKS], refs[2 * CHUNKS :]
    (gate0, gate1, up0, up1, down0, down1), refs = refs[:6], refs[6:]
    results, (tokens, active) = refs[: 2 * CHUNKS], refs[2 * CHUNKS :]
    half, chunk = results[0].shape
    hidden = gate0.shape[1]
    per_half = hidden // F_TILE
    for c in range(CHUNKS):
        for side, here, where in quarters(c, half):
            tokens[where, c * chunk : (c + 1) * chunk] = pieces[2 * c + side][here, :chunk]

    for j, (gate, up) in enumerate(((gate0, up0), (gate1, up1))):
        for i in range(per_half):
            lanes = slice(i * F_TILE, (i + 1) * F_TILE)
            gate_part = jnp.dot(tokens[...], gate[:, lanes], preferred_element_type=F32)
            up_part = jnp.dot(tokens[...], up[:, lanes], preferred_element_type=F32)
            at = j * hidden + i * F_TILE
            active[:, at : at + F_TILE] = (gate_part / (1.0 + jnp.exp(-gate_part)) * up_part).astype(BF16)

    first, chips = chip_ref[0], chip_ref[1]
    lane = lax.broadcasted_iota(jnp.int32, (half, pieces[0].shape[1] - chunk), 1)
    mine = (lane == first) | (lane == first + chips) | (lane == first + 2 * chips)
    weights = jnp.concatenate(
        [jnp.sum(jnp.where(mine, ref[:, chunk:].astype(F32), 0.0), axis=1, keepdims=True) for ref in pieces[:2]], axis=0
    )
    for n in range(CHUNKS * chunk // N_TILE):
        lanes = slice(n * N_TILE, (n + 1) * N_TILE)
        total = jnp.dot(active[:, :hidden], down0[:, lanes], preferred_element_type=F32)
        total = total + jnp.dot(active[:, hidden:], down1[:, lanes], preferred_element_type=F32)
        total = total * weights
        c, at = divmod(n * N_TILE, chunk)
        for to, here, where in quarters(c, half):
            results[2 * c + to][here, at : at + N_TILE] = total[where].astype(BF16)


def experts(chip, pieces, gates, ups, downs):
    half = pieces[0].shape[0]
    width, hidden = gates[0].shape
    vmem = pl.BlockSpec(memory_space=pltpu.VMEM)
    return pl.pallas_call(
        expert_kernel,
        out_shape=[jax.ShapeDtypeStruct((half, width // CHUNKS), BF16)] * (2 * CHUNKS),
        in_specs=[pl.BlockSpec(memory_space=pltpu.SMEM)] + [vmem] * (2 * CHUNKS + 6),
        out_specs=[vmem] * (2 * CHUNKS),
        scratch_shapes=[pltpu.VMEM((2 * half, width), BF16), pltpu.VMEM((2 * half, 2 * hidden), BF16)],
        compiler_params=pltpu.CompilerParams(vmem_limit_bytes=28 << 20),
        cost_estimate=pl.CostEstimate(flops=24 * half * width * hidden, bytes_accessed=12 * width * hidden, transcendentals=4 * half * hidden),
    )(chip, *pieces, *gates, *ups, *downs)


def normalize(hidden_state, norm_gain):
    values = [part.astype(F32) for part in hidden_state]
    square = sum(jnp.sum(part * part, axis=-1, keepdims=True) for part in values)
    scale = lax.rsqrt(square / norm_gain.size + 1e-06)
    gains = jnp.split(norm_gain, CHUNKS)
    return [(part * scale * gain).astype(BF16) for part, gain in zip(values, gains)]


def step_bits(devices):
    bits = [1 << i for i in range(1, devices.bit_length() - 1)]
    other = bits[1::-1] + bits[2:] if len(bits) > 1 else bits
    return bits, other


def swap_step(step, chunk, devices):
    orders = step_bits(devices)
    return [(i, i ^ orders[(i + chunk) & 1][step]) for i in range(devices)]


def reduce_slots(pieces, devices):
    steps = devices.bit_length() - 2
    kept, sent = list(pieces[::2]), list(pieces[1::2])
    for step in range(steps):
        for c in range(CHUNKS):
            came = lax.ppermute(sent[c], "dp", swap_step(step, c, devices))
            kept[c] = kept[c].astype(F32) + came.astype(F32)
            half = kept[c].shape[0] // 2
            if step < steps - 1:
                sent[c] = kept[c][half:].astype(BF16)
                kept[c] = kept[c][:half]
    return kept


def gather_slots(own, devices):
    own = list(own)
    steps = devices.bit_length() - 2
    pieces = []
    for step in reversed(range(steps)):
        for c in range(CHUNKS):
            came = lax.ppermute(own[c], "dp", swap_step(step, c, devices))
            if step == 0:
                pieces += [own[c], came]
            else:
                own[c] = jnp.concatenate([own[c], came], axis=0)
    return pieces


def per_device(
    residual,
    queries,
    new_kv,
    cache_kv,
    lengths,
    out_weight,
    norm_gain,
    w_gate,
    w_up,
    w_down,
    expert_ids,
    combine_weights,
):
    rows = residual.shape[0]
    devices = lax.axis_size("dp")
    chips = devices // 2
    me = lax.axis_index("dp")
    core = me % 2
    chip = me // 2
    steps = devices.bit_length() - 2
    core_swap = [(i, i ^ 1) for i in range(devices)]
    core_groups = [[2 * i + c for i in range(chips)] for c in range(2)]

    out_other = lax.ppermute(out_weight, "dp", core_swap)
    gate_other = lax.ppermute(w_gate[0], "dp", core_swap)
    up_other = lax.ppermute(w_up[0], "dp", core_swap)
    down_other = lax.ppermute(w_down[0], "dp", core_swap)

    attn_out = attend(core[None], queries, new_kv, cache_kv, lengths, chips)
    blocks = lax.all_to_all(
        attn_out, "dp", split_axis=0, concat_axis=0, axis_index_groups=core_groups, tiled=True
    )

    orders = step_bits(devices)
    slot = jnp.arange(chips, dtype=jnp.int32)
    offset = jnp.zeros_like(slot)
    for step in range(steps):
        here = jnp.where(core == 0, orders[0][step], orders[1][step]) // 2
        offset = offset + here * ((slot >> (steps - 1 - step)) & 1)
    projected = reduce_slots(project(chip ^ offset, blocks, out_weight, out_other), devices)
    hidden_state = [
        (part.astype(F32) + add).astype(BF16) for part, add in zip(jnp.split(residual, CHUNKS, axis=1), projected)
    ]
    normed = normalize(hidden_state, norm_gain)

    picks = expert_ids[:, :, None] == jnp.arange(chips, dtype=jnp.int32)
    mix = jnp.sum(jnp.where(picks, combine_weights[:, :, None], 0.0), axis=1)
    mix_hi = mix.astype(BF16)
    mix_mid = (mix - mix_hi.astype(F32)).astype(BF16)
    mix_low = (mix - mix_hi.astype(F32) - mix_mid.astype(F32)).astype(BF16)
    extra = jnp.concatenate([mix_hi, mix_mid, mix_low], axis=1)
    extra = jnp.pad(extra, ((0, 0), (0, -extra.shape[1] % 128)))
    normed, gate_other, up_other, down_other = lax.optimization_barrier((normed, gate_other, up_other, down_other))
    normed = [jnp.concatenate([normed[0], extra], axis=1)] + list(normed[1:])
    pieces = gather_slots(normed, devices)
    place = jnp.stack([chip, jnp.int32(chips)])
    outs = experts(place, pieces, (w_gate[0], gate_other), (w_up[0], up_other), (w_down[0], down_other))
    mixture = reduce_slots(outs, devices)
    return jnp.concatenate(
        [(part.astype(F32) + add).astype(BF16) for part, add in zip(hidden_state, mixture)], axis=1
    )


def solution(mesh):
    placed = (
        P(("groups", "dp"), None),
        P(("groups", "dp"), None),
        P(None, ("groups", "dp"), None),
        P(None, ("groups", "dp"), None, None),
        P(("groups", "dp")),
        P("dp", None),
        P(),
        P("dp", None, None),
        P("dp", None, None),
        P("dp", None, None),
        P(("groups", "dp"), None),
        P(("groups", "dp"), None),
    )
    return jax.shard_map(
        per_device, mesh=mesh, in_specs=placed, out_specs=P(("groups", "dp"), None), check_vma=False
    )
```

```python
import functools
import math

import jax
import jax.numpy as jnp
from jax import lax
from jax.experimental import pallas as pl
from jax.experimental.pallas import tpu as pltpu
from jax.sharding import PartitionSpec as P

H = 64
KVH = 4
DH = 128
TOP = 8
F32 = jnp.float32
BF16 = jnp.bfloat16


CHUNKS = 2


GROUP = 4


def attend_kernel(core_ref, lengths_ref, q_ref, new_ref, cache_ref, out_ref, cache, q_rows, out_rows, new_rows, sems):
    rows = q_ref.shape[0]
    heads = q_ref.shape[1] // DH
    per_group = heads // KVH
    span, width = cache_ref.shape[2:]
    scale = 1.0 / math.sqrt(DH)

    def copy(side, at):
        part = pl.ds(at * GROUP, GROUP)
        return pltpu.make_async_copy(cache_ref.at[side, part], cache.at[side, part], sems.at[side, at])

    for at in range(rows // GROUP):
        copy(0, at).start()
        copy(1, at).start()
    new_rows[...] = new_ref[...].astype(F32)
    for h in range(heads):
        q_rows[h * rows : (h + 1) * rows, :] = q_ref[:, h * DH : (h + 1) * DH].astype(F32)

    position = lax.broadcasted_iota(jnp.int32, (heads, span), 1)
    row_group = lax.broadcasted_iota(jnp.int32, (heads, width), 0) // per_group
    lane_group = lax.broadcasted_iota(jnp.int32, (heads, width), 1) // DH
    own_lanes = row_group == lane_group

    @pl.loop(0, rows // GROUP)
    def _(at):
        copy(0, at).wait()
        copy(1, at).wait()
        for i in range(GROUP):
            t = at * GROUP + i
            query = q_rows[pl.ds(t, heads, stride=rows), :]
            new_key = new_rows[0, pl.ds(t, 1), :]
            new_value = new_rows[1, pl.ds(t, 1), :]
            spread = jnp.where(own_lanes, jnp.concatenate([query] * KVH, axis=1), 0.0)
            scores = lax.dot_general(
                spread.astype(BF16), cache[0, t], (((1,), (1,)), ((), ())), preferred_element_type=F32
            )
            own = jnp.concatenate(
                [
                    jnp.sum(
                        query[g * per_group : (g + 1) * per_group] * new_key[:, g * DH : (g + 1) * DH],
                        axis=1,
                        keepdims=True,
                    )
                    for g in range(KVH)
                ],
                axis=0,
            )
            own = own * scale
            scores = jnp.where(position < lengths_ref[t], scores * scale, -1e30)
            peak = jnp.maximum(jnp.max(scores, axis=1, keepdims=True), own)
            cached_exp = jnp.exp(scores - peak)
            own_exp = jnp.exp(own - peak)
            inverse = 1.0 / (jnp.sum(cached_exp, axis=1, keepdims=True) + own_exp)
            probs = (cached_exp * inverse).astype(BF16)
            own_probs = (own_exp * inverse).astype(BF16).astype(F32)
            values = jnp.dot(probs, cache[1, t], preferred_element_type=F32)
            for g in range(KVH):
                part = slice(g * per_group, (g + 1) * per_group)
                lanes = slice(g * DH, (g + 1) * DH)
                value = values[part, lanes] + own_probs[part] * new_value[:, lanes]
                out_rows[pl.ds(g * per_group * rows + t, per_group, stride=rows), :] = value

    chips = out_ref.shape[0]
    per_chip = heads // chips
    for side in range(2):

        @pl.when(core_ref[0] == side)
        def _():
            for e in range(chips):
                for i in range(per_chip):
                    h = e * per_chip + (i + side * (per_chip // 2)) % per_chip
                    out_ref[e, :, i * DH : (i + 1) * DH] = out_rows[h * rows : (h + 1) * rows, :].astype(BF16)


def attend(core, queries, new_kv, cache_kv, lengths, chips):
    rows, features = queries.shape
    span, width = cache_kv.shape[2:]
    vmem = pl.BlockSpec(memory_space=pltpu.VMEM)
    smem = pl.BlockSpec(memory_space=pltpu.SMEM)
    return pl.pallas_call(
        attend_kernel,
        out_shape=jax.ShapeDtypeStruct((chips, rows, features // chips), BF16),
        in_specs=[smem, smem, vmem, vmem, pl.BlockSpec(memory_space=pl.ANY)],
        out_specs=vmem,
        scratch_shapes=[
            pltpu.VMEM(cache_kv.shape, BF16),
            pltpu.VMEM((features // DH * rows, DH), F32),
            pltpu.VMEM((features // DH * rows, DH), F32),
            pltpu.VMEM((2, rows, width), F32),
            pltpu.SemaphoreType.DMA((2, rows // GROUP)),
        ],
        compiler_params=pltpu.CompilerParams(vmem_limit_bytes=58 << 20),
        cost_estimate=pl.CostEstimate(flops=4 * rows * features * span, bytes_accessed=2 * cache_kv.size, transcendentals=rows * features),
    )(core, lengths, queries, new_kv, cache_kv)


P_TILE = 512


def quarters(chunk, half):
    size = half // 2
    order = (0, 2, 1, 3) if chunk % 2 else (0, 1, 2, 3)
    for place, quarter in enumerate(order):
        at = place % 2 * size
        yield place // 2, slice(at, at + size), slice(quarter * size, (quarter + 1) * size)


def project_kernel(chunk, index_ref, blocks_ref, own_ref, other_ref, keep_ref, send_ref, ordered):
    chips, rows, features = blocks_ref.shape
    half = features // 2
    for k in range(chips):
        ordered[k * rows : (k + 1) * rows, :] = blocks_ref[index_ref[k]]
    for at in range(0, keep_ref.shape[1], P_TILE):
        lanes = slice(at, at + P_TILE)
        total = jnp.dot(ordered[:, :half], own_ref[:, lanes], preferred_element_type=F32)
        total = total + jnp.dot(ordered[:, half:], other_ref[:, lanes], preferred_element_type=F32)
        for to, here, where in quarters(chunk, keep_ref.shape[0]):
            (keep_ref, send_ref)[to][here, lanes] = total[where].astype(BF16)


def whole(shape):
    return pl.BlockSpec(shape, lambda s: (0,) * len(shape))


def project(chunk, index, blocks, own, other):
    chips, rows, features = blocks.shape
    depth, width = own.shape
    size = width // CHUNKS
    weights = pl.BlockSpec((depth, size), lambda s: (0, chunk))
    half = (chips * rows // 2, size)
    return pl.pallas_call(
        functools.partial(project_kernel, chunk),
        out_shape=[jax.ShapeDtypeStruct(half, BF16)] * 2,
        grid=(1,),
        in_specs=[pl.BlockSpec(memory_space=pltpu.SMEM), whole(blocks.shape), weights, weights],
        out_specs=[whole(half)] * 2,
        scratch_shapes=[pltpu.VMEM((chips * rows, features), BF16)],
        compiler_params=pltpu.CompilerParams(vmem_limit_bytes=16 << 20),
        cost_estimate=pl.CostEstimate(flops=2 * blocks.size * size, bytes_accessed=4 * depth * size, transcendentals=0),
    )(index, blocks, own, other)


def bring_kernel(after_ref, *refs):
    count = len(refs) // 2
    sems = refs[-1]
    copies = [pltpu.make_async_copy(refs[i], refs[count + i], sems.at[i]) for i in range(count)]
    for copy in copies:
        copy.start()
    for copy in copies:
        copy.wait()


def bring(after, arrays):
    space = pl.BlockSpec(memory_space=pl.ANY)
    return pl.pallas_call(
        bring_kernel,
        out_shape=[jax.ShapeDtypeStruct(a.shape, a.dtype) for a in arrays],
        in_specs=[space] * (1 + len(arrays)),
        out_specs=[pl.BlockSpec(memory_space=pltpu.VMEM)] * len(arrays),
        scratch_shapes=[pltpu.SemaphoreType.DMA((len(arrays),))],
        compiler_params=pltpu.CompilerParams(vmem_limit_bytes=2 << 20),
        cost_estimate=pl.CostEstimate(flops=0, bytes_accessed=2 * sum(a.size for a in arrays), transcendentals=0),
    )(after, *arrays)


F_TILE = 256
N_TILE = 512


def activate(tokens_ref, gate_ref, up_ref, active_ref):
    for at in range(0, gate_ref.shape[1], F_TILE):
        lanes = slice(at, at + F_TILE)
        gate_part = jnp.dot(tokens_ref[...], gate_ref[:, lanes], preferred_element_type=F32)
        up_part = jnp.dot(tokens_ref[...], up_ref[:, lanes], preferred_element_type=F32)
        active_ref[:, lanes] = (gate_part / (1.0 + jnp.exp(-gate_part)) * up_part).astype(BF16)


def first_kernel(chip_ref, *refs):
    pieces, (gate_ref, up_ref, tokens_ref, active_ref, weights_ref) = refs[: 2 * CHUNKS], refs[2 * CHUNKS :]
    half = pieces[0].shape[0]
    chunk = tokens_ref.shape[1] // CHUNKS
    for c in range(CHUNKS):
        for side, here, where in quarters(c, half):
            tokens_ref[where, c * chunk : (c + 1) * chunk] = pieces[2 * c + side][here, :chunk]
    first, chips = chip_ref[0], chip_ref[1]
    lane = lax.broadcasted_iota(jnp.int32, (half, pieces[0].shape[1] - chunk), 1)
    mine = (lane == first) | (lane == first + chips) | (lane == first + 2 * chips)
    for side in range(2):
        weights_ref[side * half : (side + 1) * half, :] = jnp.sum(
            jnp.where(mine, pieces[side][:, chunk:].astype(F32), 0.0), axis=1, keepdims=True
        )
    activate(tokens_ref, gate_ref, up_ref, active_ref)


def down_kernel(chunk, active0, active1, weights_ref, down0, down1, keep_ref, send_ref):
    for at in range(0, keep_ref.shape[1], N_TILE):
        lanes = slice(at, at + N_TILE)
        total = jnp.dot(active0[...], down0[:, lanes], preferred_element_type=F32)
        total = total + jnp.dot(active1[...], down1[:, lanes], preferred_element_type=F32)
        total = total * weights_ref[...]
        for to, here, where in quarters(chunk, keep_ref.shape[0]):
            (keep_ref, send_ref)[to][here, lanes] = total[where].astype(BF16)


def experts(chip, pieces, gates, ups, downs):
    half = pieces[0].shape[0]
    rows = 2 * half
    width, hidden = gates[0].shape
    size = width // CHUNKS
    params = pltpu.CompilerParams(vmem_limit_bytes=20 << 20)
    cost = pl.CostEstimate(flops=4 * rows * width * hidden, bytes_accessed=4 * width * hidden, transcendentals=rows * hidden)
    vmem = pl.BlockSpec(memory_space=pltpu.VMEM)
    active = jax.ShapeDtypeStruct((rows, hidden), BF16)
    tokens, active0, weights = pl.pallas_call(
        first_kernel,
        out_shape=[jax.ShapeDtypeStruct((rows, width), BF16), active, jax.ShapeDtypeStruct((rows, 1), F32)],
        in_specs=[pl.BlockSpec(memory_space=pltpu.SMEM)] + [vmem] * (2 * CHUNKS + 2),
        out_specs=[vmem] * 3,
        compiler_params=params,
        cost_estimate=cost,
    )(chip, *pieces, gates[0], ups[0])
    active1 = pl.pallas_call(
        activate,
        out_shape=active,
        in_specs=[vmem] * 3,
        out_specs=vmem,
        compiler_params=params,
        cost_estimate=cost,
    )(tokens, gates[1], ups[1])
    results = []
    for c in range(CHUNKS):
        block = pl.BlockSpec((hidden, size), lambda s: (0, c))
        results += pl.pallas_call(
            functools.partial(down_kernel, c),
            out_shape=[jax.ShapeDtypeStruct((half, size), BF16)] * 2,
            grid=(1,),
            in_specs=[whole((rows, hidden)), whole((rows, hidden)), whole((rows, 1)), block, block],
            out_specs=[whole((half, size))] * 2,
            compiler_params=params,
            cost_estimate=pl.CostEstimate(flops=4 * rows * size * hidden, bytes_accessed=4 * size * hidden, transcendentals=0),
        )(active0, active1, weights, *downs)
    return results


def normalize(hidden_state, norm_gain):
    values = [part.astype(F32) for part in hidden_state]
    square = sum(jnp.sum(part * part, axis=-1, keepdims=True) for part in values)
    scale = lax.rsqrt(square / norm_gain.size + 1e-06)
    gains = jnp.split(norm_gain, CHUNKS)
    return [(part * scale * gain).astype(BF16) for part, gain in zip(values, gains)]


def step_bits(devices):
    bits = [1 << i for i in range(1, devices.bit_length() - 1)]
    other = bits[1::-1] + bits[2:] if len(bits) > 1 else bits
    return bits, other


def swap_step(step, chunk, devices):
    orders = step_bits(devices)
    return [(i, i ^ orders[(i + chunk) & 1][step]) for i in range(devices)]


def reduce_slots(pieces, devices):
    steps = devices.bit_length() - 2
    kept, sent = list(pieces[::2]), list(pieces[1::2])
    for step in range(steps):
        for c in range(CHUNKS):
            came = lax.ppermute(sent[c], "dp", swap_step(step, c, devices))
            kept[c] = kept[c].astype(F32) + came.astype(F32)
            half = kept[c].shape[0] // 2
            if step < steps - 1:
                sent[c] = kept[c][half:].astype(BF16)
                kept[c] = kept[c][:half]
    return kept


def gather_slots(own, devices):
    own = list(own)
    steps = devices.bit_length() - 2
    pieces = []
    for step in reversed(range(steps)):
        for c in range(CHUNKS):
            came = lax.ppermute(own[c], "dp", swap_step(step, c, devices))
            if step == 0:
                pieces += [own[c], came]
            else:
                own[c] = jnp.concatenate([own[c], came], axis=0)
    return pieces


def per_device(
    residual,
    queries,
    new_kv,
    cache_kv,
    lengths,
    out_weight,
    norm_gain,
    w_gate,
    w_up,
    w_down,
    expert_ids,
    combine_weights,
):
    rows = residual.shape[0]
    devices = lax.axis_size("dp")
    chips = devices // 2
    me = lax.axis_index("dp")
    core = me % 2
    chip = me // 2
    steps = devices.bit_length() - 2
    core_swap = [(i, i ^ 1) for i in range(devices)]
    core_groups = [[2 * i + c for i in range(chips)] for c in range(2)]

    out_other = lax.ppermute(out_weight, "dp", core_swap)
    gate_other = lax.ppermute(w_gate[0], "dp", core_swap)
    up_other = lax.ppermute(w_up[0], "dp", core_swap)
    down_other = lax.ppermute(w_down[0], "dp", core_swap)

    attn_out = attend(core[None], queries, new_kv, cache_kv, lengths, chips)
    blocks = lax.all_to_all(
        attn_out, "dp", split_axis=0, concat_axis=0, axis_index_groups=core_groups, tiled=True
    )

    orders = step_bits(devices)
    slot = jnp.arange(chips, dtype=jnp.int32)
    offset = jnp.zeros_like(slot)
    for step in range(steps):
        here = jnp.where(core == 0, orders[0][step], orders[1][step]) // 2
        offset = offset + here * ((slot >> (steps - 1 - step)) & 1)
    partial = [part for c in range(CHUNKS) for part in project(c, chip ^ offset, blocks, out_weight, out_other)]
    projected = reduce_slots(partial, devices)
    hidden_state = [
        (part.astype(F32) + add).astype(BF16) for part, add in zip(jnp.split(residual, CHUNKS, axis=1), projected)
    ]
    normed = normalize(hidden_state, norm_gain)

    picks = expert_ids[:, :, None] == jnp.arange(chips, dtype=jnp.int32)
    mix = jnp.sum(jnp.where(picks, combine_weights[:, :, None], 0.0), axis=1)
    mix_hi = mix.astype(BF16)
    mix_mid = (mix - mix_hi.astype(F32)).astype(BF16)
    mix_low = (mix - mix_hi.astype(F32) - mix_mid.astype(F32)).astype(BF16)
    extra = jnp.concatenate([mix_hi, mix_mid, mix_low], axis=1)
    extra = jnp.pad(extra, ((0, 0), (0, -extra.shape[1] % 128)))
    normed, gate_other, up_other, down_other = lax.optimization_barrier((normed, gate_other, up_other, down_other))
    normed = [jnp.concatenate([normed[0], extra], axis=1)] + list(normed[1:])
    pieces = gather_slots(normed, devices)
    gate_other, up_other, down_other = bring(pieces[2], (gate_other, up_other, down_other))
    place = jnp.stack([chip, jnp.int32(chips)])
    outs = experts(place, pieces, (w_gate[0], gate_other), (w_up[0], up_other), (w_down[0], down_other))
    mixture = reduce_slots(outs, devices)
    return jnp.concatenate(
        [(part.astype(F32) + add).astype(BF16) for part, add in zip(hidden_state, mixture)], axis=1
    )


def solution(mesh):
    placed = (
        P(("groups", "dp"), None),
        P(("groups", "dp"), None),
        P(None, ("groups", "dp"), None),
        P(None, ("groups", "dp"), None, None),
        P(("groups", "dp")),
        P("dp", None),
        P(),
        P("dp", None, None),
        P("dp", None, None),
        P("dp", None, None),
        P(("groups", "dp"), None),
        P(("groups", "dp"), None),
    )
    return jax.shard_map(
        per_device, mesh=mesh, in_specs=placed, out_specs=P(("groups", "dp"), None), check_vma=False
    )
```

```python
import functools
import math

import jax
import jax.numpy as jnp
from jax import lax
from jax.experimental import pallas as pl
from jax.experimental.pallas import tpu as pltpu
from jax.sharding import PartitionSpec as P

H = 64
KVH = 4
DH = 128
TOP = 8
F32 = jnp.float32
BF16 = jnp.bfloat16


CHUNKS = 2


GROUP = 8
PAD = 16


def attend_kernel(core_ref, lengths_ref, q_ref, new_ref, cache_ref, out_ref, cache, q_rows, out_rows, new_rows, sems):
    rows = q_ref.shape[0]
    heads = q_ref.shape[1] // DH
    per_group = heads // KVH
    span, width = cache_ref.shape[2:]
    scale = 1.0 / math.sqrt(DH)

    def copy(side, at):
        part = pl.ds(at * GROUP, GROUP)
        return pltpu.make_async_copy(cache_ref.at[side, part], cache.at[side, part, pl.ds(0, span)], sems.at[side, at])

    for at in range(rows // GROUP):
        copy(0, at).start()
        copy(1, at).start()
    new_rows[...] = new_ref[...].astype(F32)
    for h in range(heads):
        q_rows[h * rows : (h + 1) * rows, :] = q_ref[:, h * DH : (h + 1) * DH].astype(F32)

    position = lax.broadcasted_iota(jnp.int32, (span + PAD, heads), 0)
    row_group = lax.broadcasted_iota(jnp.int32, (heads, width), 0) // per_group
    lane_group = lax.broadcasted_iota(jnp.int32, (heads, width), 1) // DH
    own_lanes = row_group == lane_group

    @pl.loop(0, rows // GROUP)
    def _(at):
        copy(0, at).wait()
        copy(1, at).wait()
        scores, probs = [], []
        for i in range(GROUP):
            t = at * GROUP + i
            for side in range(2):
                cache[side, t, span:, :] = jnp.broadcast_to(new_rows[side, pl.ds(t, 1), :], (PAD, width)).astype(BF16)
            query = q_rows[pl.ds(t, heads, stride=rows), :]
            spread = jnp.where(own_lanes, jnp.concatenate([query] * KVH, axis=1), 0.0).astype(BF16)
            scores.append(
                lax.dot_general(cache[0, t], spread, (((1,), (1,)), ((), ())), preferred_element_type=F32)
            )
        for i in range(GROUP):
            live = (position < lengths_ref[at * GROUP + i]) | (position == span)
            score = jnp.where(live, scores[i] * scale, -1e30)
            weights = jnp.exp(score - jnp.max(score, axis=0, keepdims=True))
            probs.append((weights * (1.0 / jnp.sum(weights, axis=0, keepdims=True))).astype(BF16))
        for i in range(GROUP):
            t = at * GROUP + i
            values = lax.dot_general(probs[i], cache[1, t], (((0,), (0,)), ((), ())), preferred_element_type=F32)
            for g in range(KVH):
                out_rows[pl.ds(g * per_group * rows + t, per_group, stride=rows), :] = values[
                    g * per_group : (g + 1) * per_group, g * DH : (g + 1) * DH
                ]

    chips = out_ref.shape[0]
    per_chip = heads // chips
    for side in range(2):

        @pl.when(core_ref[0] == side)
        def _():
            for e in range(chips):
                for i in range(per_chip):
                    h = e * per_chip + (i + side * (per_chip // 2)) % per_chip
                    out_ref[e, :, i * DH : (i + 1) * DH] = out_rows[h * rows : (h + 1) * rows, :].astype(BF16)


def attend(core, queries, new_kv, cache_kv, lengths, chips):
    rows, features = queries.shape
    sides, _, span, width = cache_kv.shape
    vmem = pl.BlockSpec(memory_space=pltpu.VMEM)
    smem = pl.BlockSpec(memory_space=pltpu.SMEM)
    return pl.pallas_call(
        attend_kernel,
        out_shape=jax.ShapeDtypeStruct((chips, rows, features // chips), BF16),
        in_specs=[smem, smem, vmem, vmem, pl.BlockSpec(memory_space=pl.ANY)],
        out_specs=vmem,
        scratch_shapes=[
            pltpu.VMEM((sides, rows, span + PAD, width), BF16),
            pltpu.VMEM((features // DH * rows, DH), F32),
            pltpu.VMEM((features // DH * rows, DH), F32),
            pltpu.VMEM((2, rows, width), F32),
            pltpu.SemaphoreType.DMA((2, rows // GROUP)),
        ],
        compiler_params=pltpu.CompilerParams(vmem_limit_bytes=58 << 20),
        cost_estimate=pl.CostEstimate(flops=4 * rows * features * span, bytes_accessed=2 * cache_kv.size, transcendentals=rows * features),
    )(core, lengths, queries, new_kv, cache_kv)


P_TILE = 512


def quarters(chunk, half):
    size = half // 2
    order = (0, 2, 1, 3) if chunk % 2 else (0, 1, 2, 3)
    for place, quarter in enumerate(order):
        at = place % 2 * size
        yield place // 2, slice(at, at + size), slice(quarter * size, (quarter + 1) * size)


def project_kernel(chunk, index_ref, blocks_ref, own_ref, other_ref, keep_ref, send_ref, ordered):
    chips, rows, features = blocks_ref.shape
    half = features // 2
    for k in range(chips):
        ordered[k * rows : (k + 1) * rows, :] = blocks_ref[index_ref[k]]
    for at in range(0, keep_ref.shape[1], P_TILE):
        lanes = slice(at, at + P_TILE)
        total = jnp.dot(ordered[:, :half], own_ref[:, lanes], preferred_element_type=F32)
        total = total + jnp.dot(ordered[:, half:], other_ref[:, lanes], preferred_element_type=F32)
        for to, here, where in quarters(chunk, keep_ref.shape[0]):
            (keep_ref, send_ref)[to][here, lanes] = total[where].astype(BF16)


def whole(shape):
    return pl.BlockSpec(shape, lambda s: (0,) * len(shape))


def project(chunk, index, blocks, own, other):
    chips, rows, features = blocks.shape
    depth, width = own.shape
    size = width // CHUNKS
    weights = pl.BlockSpec((depth, size), lambda s: (0, chunk))
    half = (chips * rows // 2, size)
    return pl.pallas_call(
        functools.partial(project_kernel, chunk),
        out_shape=[jax.ShapeDtypeStruct(half, BF16)] * 2,
        grid=(1,),
        in_specs=[pl.BlockSpec(memory_space=pltpu.SMEM), whole(blocks.shape), weights, weights],
        out_specs=[whole(half)] * 2,
        scratch_shapes=[pltpu.VMEM((chips * rows, features), BF16)],
        compiler_params=pltpu.CompilerParams(vmem_limit_bytes=16 << 20),
        cost_estimate=pl.CostEstimate(flops=2 * blocks.size * size, bytes_accessed=4 * depth * size, transcendentals=0),
    )(index, blocks, own, other)


def bring_kernel(after_ref, *refs):
    count = len(refs) // 2
    sems = refs[-1]
    copies = [pltpu.make_async_copy(refs[i], refs[count + i], sems.at[i]) for i in range(count)]
    for copy in copies:
        copy.start()
    for copy in copies:
        copy.wait()


def bring(after, arrays):
    space = pl.BlockSpec(memory_space=pl.ANY)
    return pl.pallas_call(
        bring_kernel,
        out_shape=[jax.ShapeDtypeStruct(a.shape, a.dtype) for a in arrays],
        in_specs=[space] * (1 + len(arrays)),
        out_specs=[pl.BlockSpec(memory_space=pltpu.VMEM)] * len(arrays),
        scratch_shapes=[pltpu.SemaphoreType.DMA((len(arrays),))],
        compiler_params=pltpu.CompilerParams(vmem_limit_bytes=2 << 20),
        cost_estimate=pl.CostEstimate(flops=0, bytes_accessed=2 * sum(a.size for a in arrays), transcendentals=0),
    )(after, *arrays)


F_TILE = 256
N_TILE = 512


def activate(tokens_ref, gate_ref, up_ref, active_ref):
    for at in range(0, gate_ref.shape[1], F_TILE):
        lanes = slice(at, at + F_TILE)
        gate_part = jnp.dot(tokens_ref[...], gate_ref[:, lanes], preferred_element_type=F32)
        up_part = jnp.dot(tokens_ref[...], up_ref[:, lanes], preferred_element_type=F32)
        active_ref[:, lanes] = (gate_part / (1.0 + jnp.exp(-gate_part)) * up_part).astype(BF16)


def first_kernel(chip_ref, *refs):
    pieces, (gate_ref, up_ref, tokens_ref, active_ref, weights_ref) = refs[: 2 * CHUNKS], refs[2 * CHUNKS :]
    half = pieces[0].shape[0]
    chunk = tokens_ref.shape[1] // CHUNKS
    for c in range(CHUNKS):
        for side, here, where in quarters(c, half):
            tokens_ref[where, c * chunk : (c + 1) * chunk] = pieces[2 * c + side][here, :chunk]
    first, chips = chip_ref[0], chip_ref[1]
    lane = lax.broadcasted_iota(jnp.int32, (half, pieces[0].shape[1] - chunk), 1)
    mine = (lane == first) | (lane == first + chips) | (lane == first + 2 * chips)
    for side in range(2):
        weights_ref[side * half : (side + 1) * half, :] = jnp.sum(
            jnp.where(mine, pieces[side][:, chunk:].astype(F32), 0.0), axis=1, keepdims=True
        )
    activate(tokens_ref, gate_ref, up_ref, active_ref)


def down_kernel(chunk, active0, active1, weights_ref, down0, down1, keep_ref, send_ref):
    for at in range(0, keep_ref.shape[1], N_TILE):
        lanes = slice(at, at + N_TILE)
        total = jnp.dot(active0[...], down0[:, lanes], preferred_element_type=F32)
        total = total + jnp.dot(active1[...], down1[:, lanes], preferred_element_type=F32)
        total = total * weights_ref[...]
        for to, here, where in quarters(chunk, keep_ref.shape[0]):
            (keep_ref, send_ref)[to][here, lanes] = total[where].astype(BF16)


def experts(chip, pieces, gates, ups, downs):
    half = pieces[0].shape[0]
    rows = 2 * half
    width, hidden = gates[0].shape
    size = width // CHUNKS
    params = pltpu.CompilerParams(vmem_limit_bytes=20 << 20)
    cost = pl.CostEstimate(flops=4 * rows * width * hidden, bytes_accessed=4 * width * hidden, transcendentals=rows * hidden)
    vmem = pl.BlockSpec(memory_space=pltpu.VMEM)
    active = jax.ShapeDtypeStruct((rows, hidden), BF16)
    tokens, active0, weights = pl.pallas_call(
        first_kernel,
        out_shape=[jax.ShapeDtypeStruct((rows, width), BF16), active, jax.ShapeDtypeStruct((rows, 1), F32)],
        in_specs=[pl.BlockSpec(memory_space=pltpu.SMEM)] + [vmem] * (2 * CHUNKS + 2),
        out_specs=[vmem] * 3,
        compiler_params=params,
        cost_estimate=cost,
    )(chip, *pieces, gates[0], ups[0])
    active1 = pl.pallas_call(
        activate,
        out_shape=active,
        in_specs=[vmem] * 3,
        out_specs=vmem,
        compiler_params=params,
        cost_estimate=cost,
    )(tokens, gates[1], ups[1])
    results = []
    for c in range(CHUNKS):
        block = pl.BlockSpec((hidden, size), lambda s: (0, c))
        results += pl.pallas_call(
            functools.partial(down_kernel, c),
            out_shape=[jax.ShapeDtypeStruct((half, size), BF16)] * 2,
            grid=(1,),
            in_specs=[whole((rows, hidden)), whole((rows, hidden)), whole((rows, 1)), block, block],
            out_specs=[whole((half, size))] * 2,
            compiler_params=params,
            cost_estimate=pl.CostEstimate(flops=4 * rows * size * hidden, bytes_accessed=4 * size * hidden, transcendentals=0),
        )(active0, active1, weights, *downs)
    return results


def normalize(hidden_state, norm_gain):
    values = [part.astype(F32) for part in hidden_state]
    square = sum(jnp.sum(part * part, axis=-1, keepdims=True) for part in values)
    scale = lax.rsqrt(square / norm_gain.size + 1e-06)
    gains = jnp.split(norm_gain, CHUNKS)
    return [(part * scale * gain).astype(BF16) for part, gain in zip(values, gains)]


def step_bits(devices):
    bits = [1 << i for i in range(1, devices.bit_length() - 1)]
    other = bits[1::-1] + bits[2:] if len(bits) > 1 else bits
    return bits, other


def swap_step(step, chunk, devices):
    orders = step_bits(devices)
    return [(i, i ^ orders[(i + chunk) & 1][step]) for i in range(devices)]


def reduce_slots(pieces, devices):
    steps = devices.bit_length() - 2
    kept, sent = list(pieces[::2]), list(pieces[1::2])
    for step in range(steps):
        for c in range(CHUNKS):
            came = lax.ppermute(sent[c], "dp", swap_step(step, c, devices))
            kept[c] = kept[c].astype(F32) + came.astype(F32)
            half = kept[c].shape[0] // 2
            if step < steps - 1:
                sent[c] = kept[c][half:].astype(BF16)
                kept[c] = kept[c][:half]
    return kept


def gather_slots(own, devices):
    own = list(own)
    steps = devices.bit_length() - 2
    pieces = []
    for step in reversed(range(steps)):
        for c in range(CHUNKS):
            came = lax.ppermute(own[c], "dp", swap_step(step, c, devices))
            if step == 0:
                pieces += [own[c], came]
            else:
                own[c] = jnp.concatenate([own[c], came], axis=0)
    return pieces


def per_device(
    residual,
    queries,
    new_kv,
    cache_kv,
    lengths,
    out_weight,
    norm_gain,
    w_gate,
    w_up,
    w_down,
    expert_ids,
    combine_weights,
):
    rows = residual.shape[0]
    devices = lax.axis_size("dp")
    chips = devices // 2
    me = lax.axis_index("dp")
    core = me % 2
    chip = me // 2
    steps = devices.bit_length() - 2
    core_swap = [(i, i ^ 1) for i in range(devices)]
    core_groups = [[2 * i + c for i in range(chips)] for c in range(2)]

    out_other = lax.ppermute(out_weight, "dp", core_swap)
    gate_other = lax.ppermute(w_gate[0], "dp", core_swap)
    up_other = lax.ppermute(w_up[0], "dp", core_swap)
    down_other = lax.ppermute(w_down[0], "dp", core_swap)

    attn_out = attend(core[None], queries, new_kv, cache_kv, lengths, chips)
    (out_other,) = bring(attn_out, (out_other,))
    blocks = lax.all_to_all(
        attn_out, "dp", split_axis=0, concat_axis=0, axis_index_groups=core_groups, tiled=True
    )

    orders = step_bits(devices)
    slot = jnp.arange(chips, dtype=jnp.int32)
    offset = jnp.zeros_like(slot)
    for step in range(steps):
        here = jnp.where(core == 0, orders[0][step], orders[1][step]) // 2
        offset = offset + here * ((slot >> (steps - 1 - step)) & 1)
    partial = [part for c in range(CHUNKS) for part in project(c, chip ^ offset, blocks, out_weight, out_other)]
    projected = reduce_slots(partial, devices)
    hidden_state = [
        (part.astype(F32) + add).astype(BF16) for part, add in zip(jnp.split(residual, CHUNKS, axis=1), projected)
    ]
    normed = normalize(hidden_state, norm_gain)

    picks = expert_ids[:, :, None] == jnp.arange(chips, dtype=jnp.int32)
    mix = jnp.sum(jnp.where(picks, combine_weights[:, :, None], 0.0), axis=1)
    mix_hi = mix.astype(BF16)
    mix_mid = (mix - mix_hi.astype(F32)).astype(BF16)
    mix_low = (mix - mix_hi.astype(F32) - mix_mid.astype(F32)).astype(BF16)
    extra = jnp.concatenate([mix_hi, mix_mid, mix_low], axis=1)
    extra = jnp.pad(extra, ((0, 0), (0, -extra.shape[1] % 128)))
    normed, gate_other, up_other, down_other = lax.optimization_barrier((normed, gate_other, up_other, down_other))
    normed = [jnp.concatenate([normed[0], extra], axis=1)] + list(normed[1:])
    pieces = gather_slots(normed, devices)
    gate_other, up_other, down_other = bring(pieces[2], (gate_other, up_other, down_other))
    place = jnp.stack([chip, jnp.int32(chips)])
    outs = experts(place, pieces, (w_gate[0], gate_other), (w_up[0], up_other), (w_down[0], down_other))
    mixture = reduce_slots(outs, devices)
    return jnp.concatenate(
        [(part.astype(F32) + add).astype(BF16) for part, add in zip(hidden_state, mixture)], axis=1
    )


def solution(mesh):
    placed = (
        P(("groups", "dp"), None),
        P(("groups", "dp"), None),
        P(None, ("groups", "dp"), None),
        P(None, ("groups", "dp"), None, None),
        P(("groups", "dp")),
        P("dp", None),
        P(),
        P("dp", None, None),
        P("dp", None, None),
        P("dp", None, None),
        P(("groups", "dp"), None),
        P(("groups", "dp"), None),
    )
    return jax.shard_map(
        per_device, mesh=mesh, in_specs=placed, out_specs=P(("groups", "dp"), None), check_vma=False
    )
```

```python
import functools
import math

import jax
import jax.numpy as jnp
from jax import lax
from jax.experimental import pallas as pl
from jax.experimental.pallas import tpu as pltpu
from jax.sharding import PartitionSpec as P

H = 64
KVH = 4
DH = 128
TOP = 8
F32 = jnp.float32
BF16 = jnp.bfloat16


REDUCE = ((4, (0, 1, 2)), (4, (1, 0, 2)))
GATHER = ((3, (0, 1, 2)), (3, (1, 0, 2)), (2, (2, 0, 1)))


GROUP = 8
PAD = 16


def attend_kernel(core_ref, lengths_ref, q_ref, new_ref, cache_ref, out_ref, cache, q_rows, out_rows, new_rows, sems):
    rows = q_ref.shape[0]
    heads = q_ref.shape[1] // DH
    per_group = heads // KVH
    span, width = cache_ref.shape[2:]
    scale = 1.0 / math.sqrt(DH)

    def copy(side, at):
        part = pl.ds(at * GROUP, GROUP)
        return pltpu.make_async_copy(cache_ref.at[side, part], cache.at[side, part, pl.ds(0, span)], sems.at[side, at])

    for at in range(rows // GROUP):
        copy(0, at).start()
        copy(1, at).start()
    new_rows[...] = new_ref[...].astype(F32)
    for h in range(heads):
        q_rows[h * rows : (h + 1) * rows, :] = q_ref[:, h * DH : (h + 1) * DH].astype(F32)

    position = lax.broadcasted_iota(jnp.int32, (span + PAD, heads), 0)
    row_group = lax.broadcasted_iota(jnp.int32, (heads, width), 0) // per_group
    lane_group = lax.broadcasted_iota(jnp.int32, (heads, width), 1) // DH
    own_lanes = row_group == lane_group

    @pl.loop(0, rows // GROUP)
    def _(at):
        copy(0, at).wait()
        copy(1, at).wait()
        scores, probs = [], []
        for i in range(GROUP):
            t = at * GROUP + i
            for side in range(2):
                cache[side, t, span:, :] = jnp.broadcast_to(new_rows[side, pl.ds(t, 1), :], (PAD, width)).astype(BF16)
            query = q_rows[pl.ds(t, heads, stride=rows), :]
            spread = jnp.where(own_lanes, jnp.concatenate([query] * KVH, axis=1), 0.0).astype(BF16)
            scores.append(
                lax.dot_general(cache[0, t], spread, (((1,), (1,)), ((), ())), preferred_element_type=F32)
            )
        for i in range(GROUP):
            live = (position < lengths_ref[at * GROUP + i]) | (position == span)
            score = jnp.where(live, scores[i] * scale, -1e30)
            weights = jnp.exp(score - jnp.max(score, axis=0, keepdims=True))
            probs.append((weights * (1.0 / jnp.sum(weights, axis=0, keepdims=True))).astype(BF16))
        for i in range(GROUP):
            t = at * GROUP + i
            values = lax.dot_general(probs[i], cache[1, t], (((0,), (0,)), ((), ())), preferred_element_type=F32)
            for g in range(KVH):
                out_rows[pl.ds(g * per_group * rows + t, per_group, stride=rows), :] = values[
                    g * per_group : (g + 1) * per_group, g * DH : (g + 1) * DH
                ]

    chips = out_ref.shape[0]
    per_chip = heads // chips
    for side in range(2):

        @pl.when(core_ref[0] == side)
        def _():
            for e in range(chips):
                for i in range(per_chip):
                    h = e * per_chip + (i + side * (per_chip // 2)) % per_chip
                    out_ref[e, :, i * DH : (i + 1) * DH] = out_rows[h * rows : (h + 1) * rows, :].astype(BF16)


def attend(core, queries, new_kv, cache_kv, lengths, chips):
    rows, features = queries.shape
    sides, _, span, width = cache_kv.shape
    vmem = pl.BlockSpec(memory_space=pltpu.VMEM)
    smem = pl.BlockSpec(memory_space=pltpu.SMEM)
    return pl.pallas_call(
        attend_kernel,
        out_shape=jax.ShapeDtypeStruct((chips, rows, features // chips), BF16),
        in_specs=[smem, smem, vmem, vmem, pl.BlockSpec(memory_space=pl.ANY)],
        out_specs=vmem,
        scratch_shapes=[
            pltpu.VMEM((sides, rows, span + PAD, width), BF16),
            pltpu.VMEM((features // DH * rows, DH), F32),
            pltpu.VMEM((features // DH * rows, DH), F32),
            pltpu.VMEM((2, rows, width), F32),
            pltpu.SemaphoreType.DMA((2, rows // GROUP)),
        ],
        compiler_params=pltpu.CompilerParams(vmem_limit_bytes=58 << 20),
        cost_estimate=pl.CostEstimate(flops=4 * rows * features * span, bytes_accessed=2 * cache_kv.size, transcendentals=rows * features),
    )(core, lengths, queries, new_kv, cache_kv)


P_TILE = 512


def spans(chunks, width):
    at = 0
    for eighths, order in chunks:
        size = width * eighths // 8
        yield at, size, order
        at += size


def octants(order, half):
    size = half // 4
    for place in range(8):
        base = sum((place >> (2 - step) & 1) << (2 - order[step]) for step in range(3))
        at = place % 4 * size
        yield place // 4, slice(at, at + size), slice(base * size, (base + 1) * size)


def project_kernel(order, after_ref, index_ref, blocks_ref, own_ref, other_ref, keep_ref, send_ref, ordered):
    chips, rows, features = blocks_ref.shape
    half = features // 2
    for k in range(chips):
        ordered[k * rows : (k + 1) * rows, :] = blocks_ref[index_ref[k]]
    for at in range(0, keep_ref.shape[1], P_TILE):
        lanes = slice(at, at + P_TILE)
        total = jnp.dot(ordered[:, :half], own_ref[:, lanes], preferred_element_type=F32)
        total = total + jnp.dot(ordered[:, half:], other_ref[:, lanes], preferred_element_type=F32)
        for to, here, where in octants(order, keep_ref.shape[0]):
            (keep_ref, send_ref)[to][here, lanes] = total[where].astype(BF16)


def whole(shape):
    return pl.BlockSpec(shape, lambda s: (0,) * len(shape))


def project(span, after, index, blocks, own, other):
    chips, rows, features = blocks.shape
    depth = own.shape[0]
    first, size, order = span
    weights = pl.BlockSpec((depth, size), lambda s: (0, first // size))
    half = (chips * rows // 2, size)
    return pl.pallas_call(
        functools.partial(project_kernel, order),
        out_shape=[jax.ShapeDtypeStruct(half, BF16)] * 2,
        grid=(1,),
        in_specs=[
            pl.BlockSpec(memory_space=pl.ANY),
            pl.BlockSpec(memory_space=pltpu.SMEM),
            whole(blocks.shape),
            weights,
            weights,
        ],
        out_specs=[whole(half)] * 2,
        scratch_shapes=[pltpu.VMEM((chips * rows, features), BF16)],
        compiler_params=pltpu.CompilerParams(vmem_limit_bytes=16 << 20),
        cost_estimate=pl.CostEstimate(flops=2 * blocks.size * size, bytes_accessed=4 * depth * size, transcendentals=0),
    )(after, index, blocks, own, other)


def bring_kernel(after_ref, *refs):
    count = len(refs) // 2
    sems = refs[-1]
    copies = [pltpu.make_async_copy(refs[i], refs[count + i], sems.at[i]) for i in range(count)]
    for copy in copies:
        copy.start()
    for copy in copies:
        copy.wait()


def bring(after, arrays):
    space = pl.BlockSpec(memory_space=pl.ANY)
    return pl.pallas_call(
        bring_kernel,
        out_shape=[jax.ShapeDtypeStruct(a.shape, a.dtype) for a in arrays],
        in_specs=[space] * (1 + len(arrays)),
        out_specs=[pl.BlockSpec(memory_space=pltpu.VMEM)] * len(arrays),
        scratch_shapes=[pltpu.SemaphoreType.DMA((len(arrays),))],
        compiler_params=pltpu.CompilerParams(vmem_limit_bytes=2 << 20),
        cost_estimate=pl.CostEstimate(flops=0, bytes_accessed=2 * sum(a.size for a in arrays), transcendentals=0),
    )(after, *arrays)


F_TILE = 256
N_TILE = 512


def activate(tokens_ref, gate_ref, up_ref, active_ref):
    for at in range(0, gate_ref.shape[1], F_TILE):
        lanes = slice(at, at + F_TILE)
        gate_part = jnp.dot(tokens_ref[...], gate_ref[:, lanes], preferred_element_type=F32)
        up_part = jnp.dot(tokens_ref[...], up_ref[:, lanes], preferred_element_type=F32)
        active_ref[:, lanes] = (gate_part / (1.0 + jnp.exp(-gate_part)) * up_part).astype(BF16)


def first_kernel(chip_ref, *refs):
    pieces, (gate_ref, up_ref, tokens_ref, active_ref, weights_ref) = refs[:-5], refs[-5:]
    half = pieces[0].shape[0]
    for c, (at, size, order) in enumerate(spans(GATHER, tokens_ref.shape[1])):
        for side, here, where in octants(order, half):
            tokens_ref[where, at : at + size] = pieces[2 * c + side][here, :size]
    chunk = GATHER[0][0] * tokens_ref.shape[1] // 8
    first, chips = chip_ref[0], chip_ref[1]
    lane = lax.broadcasted_iota(jnp.int32, (half, pieces[0].shape[1] - chunk), 1)
    mine = (lane == first) | (lane == first + chips) | (lane == first + 2 * chips)
    for side in range(2):
        weights_ref[side * half : (side + 1) * half, :] = jnp.sum(
            jnp.where(mine, pieces[side][:, chunk:].astype(F32), 0.0), axis=1, keepdims=True
        )
    activate(tokens_ref, gate_ref, up_ref, active_ref)


def down_kernel(order, after_ref, active0, active1, weights_ref, down0, down1, keep_ref, send_ref):
    for at in range(0, keep_ref.shape[1], N_TILE):
        lanes = slice(at, at + N_TILE)
        total = jnp.dot(active0[...], down0[:, lanes], preferred_element_type=F32)
        total = total + jnp.dot(active1[...], down1[:, lanes], preferred_element_type=F32)
        total = total * weights_ref[...]
        for to, here, where in octants(order, keep_ref.shape[0]):
            (keep_ref, send_ref)[to][here, lanes] = total[where].astype(BF16)


def experts(chip, pieces, gates, ups, downs):
    half = pieces[0].shape[0]
    rows = 2 * half
    width, hidden = gates[0].shape
    params = pltpu.CompilerParams(vmem_limit_bytes=20 << 20)
    cost = pl.CostEstimate(flops=4 * rows * width * hidden, bytes_accessed=4 * width * hidden, transcendentals=rows * hidden)
    vmem = pl.BlockSpec(memory_space=pltpu.VMEM)
    active = jax.ShapeDtypeStruct((rows, hidden), BF16)
    tokens, active0, weights = pl.pallas_call(
        first_kernel,
        out_shape=[jax.ShapeDtypeStruct((rows, width), BF16), active, jax.ShapeDtypeStruct((rows, 1), F32)],
        in_specs=[pl.BlockSpec(memory_space=pltpu.SMEM)] + [vmem] * (len(pieces) + 2),
        out_specs=[vmem] * 3,
        compiler_params=params,
        cost_estimate=cost,
    )(chip, *pieces, gates[0], ups[0])
    active1 = pl.pallas_call(
        activate,
        out_shape=active,
        in_specs=[vmem] * 3,
        out_specs=vmem,
        compiler_params=params,
        cost_estimate=cost,
    )(tokens, gates[1], ups[1])
    results = []
    for first, size, order in spans(REDUCE, width):
        block = pl.BlockSpec((hidden, size), functools.partial(lambda s, index: (0, index), index=first // size))
        results += pl.pallas_call(
            functools.partial(down_kernel, order),
            out_shape=[jax.ShapeDtypeStruct((half, size), BF16)] * 2,
            grid=(1,),
            in_specs=[pl.BlockSpec(memory_space=pl.ANY), whole((rows, hidden)), whole((rows, hidden)), whole((rows, 1))]
            + [block, block],
            out_specs=[whole((half, size))] * 2,
            compiler_params=params,
            cost_estimate=pl.CostEstimate(flops=4 * rows * size * hidden, bytes_accessed=4 * size * hidden, transcendentals=0),
        )(results[-1] if results else active1, active0, active1, weights, *downs)
    return results


def normalize(hidden_state, norm_gain):
    values = [part.astype(F32) for part in hidden_state]
    square = sum(jnp.sum(part * part, axis=-1, keepdims=True) for part in values)
    scale = lax.rsqrt(square / norm_gain.size + 1e-06)
    gains = [norm_gain[at : at + size] for at, size, _ in spans(REDUCE, norm_gain.size)]
    return [(part * scale * gain).astype(BF16) for part, gain in zip(values, gains)]


def step_bits(devices, order=(0, 1, 2)):
    even = [1 << i for i in range(1, devices.bit_length() - 1)]
    odd = even[1::-1] + even[2:]
    return [[bits[i] for i in order] + bits[3:] for bits in (even, odd)]


def swap_step(step, order, devices):
    orders = step_bits(devices, order)
    return [(i, i ^ orders[i & 1][step]) for i in range(devices)]


def reduce_slots(pieces, devices):
    steps = devices.bit_length() - 2
    kept, sent = list(pieces[::2]), list(pieces[1::2])
    for step in range(steps):
        for c, (_, order) in enumerate(REDUCE):
            came = lax.ppermute(sent[c], "dp", swap_step(step, order, devices))
            kept[c] = kept[c].astype(F32) + came.astype(F32)
            half = kept[c].shape[0] // 2
            if step < steps - 1:
                sent[c] = kept[c][half:].astype(BF16)
                kept[c] = kept[c][:half]
    return kept


def gather_slots(own, devices):
    own = list(own)
    steps = devices.bit_length() - 2
    pieces = []
    for step in reversed(range(steps)):
        for c, (_, order) in enumerate(GATHER):
            came = lax.ppermute(own[c], "dp", swap_step(step, order, devices))
            if step == 0:
                pieces += [own[c], came]
            else:
                own[c] = jnp.concatenate([own[c], came], axis=0)
    return pieces


def per_device(
    residual,
    queries,
    new_kv,
    cache_kv,
    lengths,
    out_weight,
    norm_gain,
    w_gate,
    w_up,
    w_down,
    expert_ids,
    combine_weights,
):
    rows, width = residual.shape
    devices = lax.axis_size("dp")
    chips = devices // 2
    me = lax.axis_index("dp")
    core = me % 2
    chip = me // 2
    steps = devices.bit_length() - 2
    core_swap = [(i, i ^ 1) for i in range(devices)]
    core_groups = [[2 * i + c for i in range(chips)] for c in range(2)]

    out_other = lax.ppermute(out_weight, "dp", core_swap)
    gate_other = lax.ppermute(w_gate[0], "dp", core_swap)
    up_other = lax.ppermute(w_up[0], "dp", core_swap)
    down_other = lax.ppermute(w_down[0], "dp", core_swap)

    attn_out = attend(core[None], queries, new_kv, cache_kv, lengths, chips)
    out_own, out_other = bring(attn_out, (out_weight, out_other))
    blocks = lax.all_to_all(
        attn_out, "dp", split_axis=0, concat_axis=0, axis_index_groups=core_groups, tiled=True
    )

    orders = step_bits(devices)
    slot = jnp.arange(chips, dtype=jnp.int32)
    offset = jnp.zeros_like(slot)
    for step in range(steps):
        here = jnp.where(core == 0, orders[0][step], orders[1][step]) // 2
        offset = offset + here * ((slot >> (steps - 1 - step)) & 1)
    cuts = list(spans(REDUCE, width))
    partial = []
    for span in cuts:
        partial += project(span, partial[-1] if partial else blocks, chip ^ offset, blocks, out_own, out_other)
    projected = reduce_slots(partial, devices)
    hidden_state = [
        (residual[:, at : at + size].astype(F32) + add).astype(BF16) for (at, size, _), add in zip(cuts, projected)
    ]
    normed = normalize(hidden_state, norm_gain)

    picks = expert_ids[:, :, None] == jnp.arange(chips, dtype=jnp.int32)
    mix = jnp.sum(jnp.where(picks, combine_weights[:, :, None], 0.0), axis=1)
    mix_hi = mix.astype(BF16)
    mix_mid = (mix - mix_hi.astype(F32)).astype(BF16)
    mix_low = (mix - mix_hi.astype(F32) - mix_mid.astype(F32)).astype(BF16)
    extra = jnp.concatenate([mix_hi, mix_mid, mix_low], axis=1)
    extra = jnp.pad(extra, ((0, 0), (0, -extra.shape[1] % 128)))
    normed, gate_other, up_other, down_other = lax.optimization_barrier((normed, gate_other, up_other, down_other))
    normed = jnp.concatenate(normed, axis=1)
    normed = [normed[:, at : at + size] for at, size, _ in spans(GATHER, width)]
    normed[0] = jnp.concatenate([normed[0], extra], axis=1)
    pieces = gather_slots(normed, devices)
    gate_other, up_other, down_other = bring(pieces[-2], (gate_other, up_other, down_other))
    place = jnp.stack([chip, jnp.int32(chips)])
    outs = experts(place, pieces, (w_gate[0], gate_other), (w_up[0], up_other), (w_down[0], down_other))
    mixture = reduce_slots(outs, devices)
    return jnp.concatenate(
        [(part.astype(F32) + add).astype(BF16) for part, add in zip(hidden_state, mixture)], axis=1
    )


def solution(mesh):
    placed = (
        P(("groups", "dp"), None),
        P(("groups", "dp"), None),
        P(None, ("groups", "dp"), None),
        P(None, ("groups", "dp"), None, None),
        P(("groups", "dp")),
        P("dp", None),
        P(),
        P("dp", None, None),
        P("dp", None, None),
        P("dp", None, None),
        P(("groups", "dp"), None),
        P(("groups", "dp"), None),
    )
    return jax.shard_map(
        per_device, mesh=mesh, in_specs=placed, out_specs=P(("groups", "dp"), None), check_vma=False
    )
```

```python
import functools
import math

import jax
import jax.numpy as jnp
from jax import lax
from jax.experimental import pallas as pl
from jax.experimental.pallas import tpu as pltpu
from jax.sharding import PartitionSpec as P

H = 64
KVH = 4
DH = 128
TOP = 8
F32 = jnp.float32
BF16 = jnp.bfloat16


REDUCE = ((4, (0, 1, 2)), (4, (1, 2, 0)))
GATHER = ((3, (0, 1, 2)), (3, (1, 0, 2)), (2, (2, 0, 1)))


GROUP = 8
PAD = 16


def attend_kernel(core_ref, lengths_ref, q_ref, new_ref, cache_ref, out_ref, cache, q_rows, out_rows, new_rows, sems):
    rows = q_ref.shape[0]
    heads = q_ref.shape[1] // DH
    per_group = heads // KVH
    span, width = cache_ref.shape[2:]
    scale = 1.0 / math.sqrt(DH)

    def copy(side, at):
        part = pl.ds(at * GROUP, GROUP)
        return pltpu.make_async_copy(cache_ref.at[side, part], cache.at[side, part, pl.ds(0, span)], sems.at[side, at])

    for at in range(rows // GROUP):
        copy(0, at).start()
        copy(1, at).start()
    new_rows[...] = new_ref[...].astype(F32)
    for h in range(heads):
        q_rows[h * rows : (h + 1) * rows, :] = q_ref[:, h * DH : (h + 1) * DH].astype(F32)

    position = lax.broadcasted_iota(jnp.int32, (span + PAD, heads), 0)
    row_group = lax.broadcasted_iota(jnp.int32, (heads, width), 0) // per_group
    lane_group = lax.broadcasted_iota(jnp.int32, (heads, width), 1) // DH
    own_lanes = row_group == lane_group

    @pl.loop(0, rows // GROUP)
    def _(at):
        copy(0, at).wait()
        copy(1, at).wait()
        scores, probs = [], []
        for i in range(GROUP):
            t = at * GROUP + i
            for side in range(2):
                cache[side, t, span:, :] = jnp.broadcast_to(new_rows[side, pl.ds(t, 1), :], (PAD, width)).astype(BF16)
            query = q_rows[pl.ds(t, heads, stride=rows), :]
            spread = jnp.where(own_lanes, jnp.concatenate([query] * KVH, axis=1), 0.0).astype(BF16)
            scores.append(
                lax.dot_general(cache[0, t], spread, (((1,), (1,)), ((), ())), preferred_element_type=F32)
            )
        for i in range(GROUP):
            live = (position < lengths_ref[at * GROUP + i]) | (position == span)
            score = jnp.where(live, scores[i] * scale, -1e30)
            weights = jnp.exp(score - jnp.max(score, axis=0, keepdims=True))
            probs.append((weights * (1.0 / jnp.sum(weights, axis=0, keepdims=True))).astype(BF16))
        for i in range(GROUP):
            t = at * GROUP + i
            values = lax.dot_general(probs[i], cache[1, t], (((0,), (0,)), ((), ())), preferred_element_type=F32)
            for g in range(KVH):
                out_rows[pl.ds(g * per_group * rows + t, per_group, stride=rows), :] = values[
                    g * per_group : (g + 1) * per_group, g * DH : (g + 1) * DH
                ]

    chips = out_ref.shape[0]
    per_chip = heads // chips
    for side in range(2):

        @pl.when(core_ref[0] == side)
        def _():
            for e in range(chips):
                for i in range(per_chip):
                    h = e * per_chip + (i + side * (per_chip // 2)) % per_chip
                    out_ref[e, :, i * DH : (i + 1) * DH] = out_rows[h * rows : (h + 1) * rows, :].astype(BF16)


def attend(core, queries, new_kv, cache_kv, lengths, chips):
    rows, features = queries.shape
    sides, _, span, width = cache_kv.shape
    vmem = pl.BlockSpec(memory_space=pltpu.VMEM)
    smem = pl.BlockSpec(memory_space=pltpu.SMEM)
    return pl.pallas_call(
        attend_kernel,
        out_shape=jax.ShapeDtypeStruct((chips, rows, features // chips), BF16),
        in_specs=[smem, smem, vmem, vmem, pl.BlockSpec(memory_space=pl.ANY)],
        out_specs=vmem,
        scratch_shapes=[
            pltpu.VMEM((sides, rows, span + PAD, width), BF16),
            pltpu.VMEM((features // DH * rows, DH), F32),
            pltpu.VMEM((features // DH * rows, DH), F32),
            pltpu.VMEM((2, rows, width), F32),
            pltpu.SemaphoreType.DMA((2, rows // GROUP)),
        ],
        compiler_params=pltpu.CompilerParams(vmem_limit_bytes=58 << 20),
        cost_estimate=pl.CostEstimate(flops=4 * rows * features * span, bytes_accessed=2 * cache_kv.size, transcendentals=rows * features),
    )(core, lengths, queries, new_kv, cache_kv)


P_TILE = 512


def spans(chunks, width):
    at = 0
    for eighths, order in chunks:
        size = width * eighths // 8
        yield at, size, order
        at += size


def octants(order, half):
    size = half // 4
    for place in range(8):
        base = sum((place >> (2 - step) & 1) << (2 - order[step]) for step in range(3))
        at = place % 4 * size
        yield place // 4, slice(at, at + size), slice(base * size, (base + 1) * size)


def project_kernel(order, index_ref, blocks_ref, own_ref, other_ref, keep_ref, send_ref, ordered):
    chips, rows, features = blocks_ref.shape
    half = features // 2
    for k in range(chips):
        ordered[k * rows : (k + 1) * rows, :] = blocks_ref[index_ref[k]]
    for at in range(0, keep_ref.shape[1], P_TILE):
        lanes = slice(at, at + P_TILE)
        total = jnp.dot(ordered[:, :half], own_ref[:, lanes], preferred_element_type=F32)
        total = total + jnp.dot(ordered[:, half:], other_ref[:, lanes], preferred_element_type=F32)
        for to, here, where in octants(order, keep_ref.shape[0]):
            (keep_ref, send_ref)[to][here, lanes] = total[where].astype(BF16)


def whole(shape):
    return pl.BlockSpec(shape, lambda s: (0,) * len(shape))


def project(span, index, blocks, own, other):
    chips, rows, features = blocks.shape
    depth = own.shape[0]
    first, size, order = span
    weights = pl.BlockSpec((depth, size), lambda s: (0, first // size))
    half = (chips * rows // 2, size)
    return pl.pallas_call(
        functools.partial(project_kernel, order),
        out_shape=[jax.ShapeDtypeStruct(half, BF16)] * 2,
        grid=(1,),
        in_specs=[
            pl.BlockSpec(memory_space=pltpu.SMEM),
            whole(blocks.shape),
            weights,
            weights,
        ],
        out_specs=[whole(half)] * 2,
        scratch_shapes=[pltpu.VMEM((chips * rows, features), BF16)],
        compiler_params=pltpu.CompilerParams(vmem_limit_bytes=16 << 20),
        cost_estimate=pl.CostEstimate(flops=2 * blocks.size * size, bytes_accessed=4 * depth * size, transcendentals=0),
    )(index, blocks, own, other)


def bring_kernel(after_ref, *refs):
    count = len(refs) // 2
    sems = refs[-1]
    copies = [pltpu.make_async_copy(refs[i], refs[count + i], sems.at[i]) for i in range(count)]
    for copy in copies:
        copy.start()
    for copy in copies:
        copy.wait()


def bring(after, arrays):
    space = pl.BlockSpec(memory_space=pl.ANY)
    return pl.pallas_call(
        bring_kernel,
        out_shape=[jax.ShapeDtypeStruct(a.shape, a.dtype) for a in arrays],
        in_specs=[space] * (1 + len(arrays)),
        out_specs=[pl.BlockSpec(memory_space=pltpu.VMEM)] * len(arrays),
        scratch_shapes=[pltpu.SemaphoreType.DMA((len(arrays),))],
        compiler_params=pltpu.CompilerParams(vmem_limit_bytes=2 << 20),
        cost_estimate=pl.CostEstimate(flops=0, bytes_accessed=2 * sum(a.size for a in arrays), transcendentals=0),
    )(after, *arrays)


F_TILE = 256
N_TILE = 512


def activate(tokens_ref, gate_ref, up_ref, active_ref):
    for at in range(0, gate_ref.shape[1], F_TILE):
        lanes = slice(at, at + F_TILE)
        gate_part = jnp.dot(tokens_ref[...], gate_ref[:, lanes], preferred_element_type=F32)
        up_part = jnp.dot(tokens_ref[...], up_ref[:, lanes], preferred_element_type=F32)
        active_ref[:, lanes] = (gate_part / (1.0 + jnp.exp(-gate_part)) * up_part).astype(BF16)


def first_kernel(chip_ref, *refs):
    pieces, (gate_ref, up_ref, tokens_ref, active_ref, weights_ref) = refs[:-5], refs[-5:]
    half = pieces[0].shape[0]
    for c, (at, size, order) in enumerate(spans(GATHER, tokens_ref.shape[1])):
        for side, here, where in octants(order, half):
            tokens_ref[where, at : at + size] = pieces[2 * c + side][here, :size]
    chunk = GATHER[0][0] * tokens_ref.shape[1] // 8
    first, chips = chip_ref[0], chip_ref[1]
    lane = lax.broadcasted_iota(jnp.int32, (half, pieces[0].shape[1] - chunk), 1)
    mine = (lane == first) | (lane == first + chips) | (lane == first + 2 * chips)
    for side in range(2):
        weights_ref[side * half : (side + 1) * half, :] = jnp.sum(
            jnp.where(mine, pieces[side][:, chunk:].astype(F32), 0.0), axis=1, keepdims=True
        )
    activate(tokens_ref, gate_ref, up_ref, active_ref)


def down_kernel(order, after_ref, active0, active1, weights_ref, down0, down1, keep_ref, send_ref):
    for at in range(0, keep_ref.shape[1], N_TILE):
        lanes = slice(at, at + N_TILE)
        total = jnp.dot(active0[...], down0[:, lanes], preferred_element_type=F32)
        total = total + jnp.dot(active1[...], down1[:, lanes], preferred_element_type=F32)
        total = total * weights_ref[...]
        for to, here, where in octants(order, keep_ref.shape[0]):
            (keep_ref, send_ref)[to][here, lanes] = total[where].astype(BF16)


def experts(chip, pieces, gates, ups, downs):
    half = pieces[0].shape[0]
    rows = 2 * half
    width, hidden = gates[0].shape
    params = pltpu.CompilerParams(vmem_limit_bytes=20 << 20)
    cost = pl.CostEstimate(flops=4 * rows * width * hidden, bytes_accessed=4 * width * hidden, transcendentals=rows * hidden)
    vmem = pl.BlockSpec(memory_space=pltpu.VMEM)
    active = jax.ShapeDtypeStruct((rows, hidden), BF16)
    tokens, active0, weights = pl.pallas_call(
        first_kernel,
        out_shape=[jax.ShapeDtypeStruct((rows, width), BF16), active, jax.ShapeDtypeStruct((rows, 1), F32)],
        in_specs=[pl.BlockSpec(memory_space=pltpu.SMEM)] + [vmem] * (len(pieces) + 2),
        out_specs=[vmem] * 3,
        compiler_params=params,
        cost_estimate=cost,
    )(chip, *pieces, gates[0], ups[0])
    active1 = pl.pallas_call(
        activate,
        out_shape=active,
        in_specs=[vmem] * 3,
        out_specs=vmem,
        compiler_params=params,
        cost_estimate=cost,
    )(tokens, gates[1], ups[1])
    results = []
    for first, size, order in spans(REDUCE, width):
        block = pl.BlockSpec((hidden, size), functools.partial(lambda s, index: (0, index), index=first // size))
        results += pl.pallas_call(
            functools.partial(down_kernel, order),
            out_shape=[jax.ShapeDtypeStruct((half, size), BF16)] * 2,
            grid=(1,),
            in_specs=[pl.BlockSpec(memory_space=pl.ANY), whole((rows, hidden)), whole((rows, hidden)), whole((rows, 1))]
            + [block, block],
            out_specs=[whole((half, size))] * 2,
            compiler_params=params,
            cost_estimate=pl.CostEstimate(flops=4 * rows * size * hidden, bytes_accessed=4 * size * hidden, transcendentals=0),
        )(results[-1] if results else active1, active0, active1, weights, *downs)
    return results


def normalize(hidden_state, norm_gain):
    values = [part.astype(F32) for part in hidden_state]
    square = sum(jnp.sum(part * part, axis=-1, keepdims=True) for part in values)
    scale = lax.rsqrt(square / norm_gain.size + 1e-06)
    gains = [norm_gain[at : at + size] for at, size, _ in spans(REDUCE, norm_gain.size)]
    return [(part * scale * gain).astype(BF16) for part, gain in zip(values, gains)]


def step_bits(devices, order=(0, 1, 2)):
    even = [1 << i for i in range(1, devices.bit_length() - 1)]
    odd = [even[i] for i in (2, 0, 1)] + even[3:]
    return [[bits[i] for i in order] + bits[3:] for bits in (even, odd)]


def swap_step(step, order, devices):
    orders = step_bits(devices, order)
    return [(i, i ^ orders[i & 1][step]) for i in range(devices)]


def reduce_slots(pieces, devices):
    steps = devices.bit_length() - 2
    kept, sent = list(pieces[::2]), list(pieces[1::2])
    for step in range(steps):
        for c, (_, order) in enumerate(REDUCE):
            came = lax.ppermute(sent[c], "dp", swap_step(step, order, devices))
            kept[c] = kept[c].astype(F32) + came.astype(F32)
            half = kept[c].shape[0] // 2
            if step < steps - 1:
                sent[c] = kept[c][half:].astype(BF16)
                kept[c] = kept[c][:half]
    return kept


def gather_slots(own, devices):
    own = list(own)
    steps = devices.bit_length() - 2
    pieces = []
    for step in reversed(range(steps)):
        for c, (_, order) in enumerate(GATHER):
            came = lax.ppermute(own[c], "dp", swap_step(step, order, devices))
            if step == 0:
                pieces += [own[c], came]
            else:
                own[c] = jnp.concatenate([own[c], came], axis=0)
    return pieces


def per_device(
    residual,
    queries,
    new_kv,
    cache_kv,
    lengths,
    out_weight,
    norm_gain,
    w_gate,
    w_up,
    w_down,
    expert_ids,
    combine_weights,
):
    rows, width = residual.shape
    devices = lax.axis_size("dp")
    chips = devices // 2
    me = lax.axis_index("dp")
    core = me % 2
    chip = me // 2
    steps = devices.bit_length() - 2
    core_swap = [(i, i ^ 1) for i in range(devices)]
    core_groups = [[2 * i + c for i in range(chips)] for c in range(2)]

    out_other = lax.ppermute(out_weight, "dp", core_swap)
    gate_other = lax.ppermute(w_gate[0], "dp", core_swap)
    up_other = lax.ppermute(w_up[0], "dp", core_swap)
    down_other = lax.ppermute(w_down[0], "dp", core_swap)

    attn_out = attend(core[None], queries, new_kv, cache_kv, lengths, chips)
    blocks = lax.all_to_all(
        attn_out, "dp", split_axis=0, concat_axis=0, axis_index_groups=core_groups, tiled=True
    )

    orders = step_bits(devices)
    slot = jnp.arange(chips, dtype=jnp.int32)
    offset = jnp.zeros_like(slot)
    for step in range(steps):
        here = jnp.where(core == 0, orders[0][step], orders[1][step]) // 2
        offset = offset + here * ((slot >> (steps - 1 - step)) & 1)
    cuts = list(spans(REDUCE, width))
    partial = []
    for span in cuts:
        partial += project(span, chip ^ offset, blocks, out_weight, out_other)
    projected = reduce_slots(partial, devices)
    hidden_state = [
        (residual[:, at : at + size].astype(F32) + add).astype(BF16) for (at, size, _), add in zip(cuts, projected)
    ]
    normed = normalize(hidden_state, norm_gain)

    picks = expert_ids[:, :, None] == jnp.arange(chips, dtype=jnp.int32)
    mix = jnp.sum(jnp.where(picks, combine_weights[:, :, None], 0.0), axis=1)
    mix_hi = mix.astype(BF16)
    mix_mid = (mix - mix_hi.astype(F32)).astype(BF16)
    mix_low = (mix - mix_hi.astype(F32) - mix_mid.astype(F32)).astype(BF16)
    extra = jnp.concatenate([mix_hi, mix_mid, mix_low], axis=1)
    extra = jnp.pad(extra, ((0, 0), (0, -extra.shape[1] % 128)))
    normed, gate_other, up_other, down_other = lax.optimization_barrier((normed, gate_other, up_other, down_other))
    normed = jnp.concatenate(normed, axis=1)
    normed = [normed[:, at : at + size] for at, size, _ in spans(GATHER, width)]
    normed[0] = jnp.concatenate([normed[0], extra], axis=1)
    pieces = gather_slots(normed, devices)
    gate_other, up_other, down_other = bring(pieces[-2], (gate_other, up_other, down_other))
    place = jnp.stack([chip, jnp.int32(chips)])
    outs = experts(place, pieces, (w_gate[0], gate_other), (w_up[0], up_other), (w_down[0], down_other))
    mixture = reduce_slots(outs, devices)
    return jnp.concatenate(
        [(part.astype(F32) + add).astype(BF16) for part, add in zip(hidden_state, mixture)], axis=1
    )


def solution(mesh):
    placed = (
        P(("groups", "dp"), None),
        P(("groups", "dp"), None),
        P(None, ("groups", "dp"), None),
        P(None, ("groups", "dp"), None, None),
        P(("groups", "dp")),
        P("dp", None),
        P(),
        P("dp", None, None),
        P("dp", None, None),
        P("dp", None, None),
        P(("groups", "dp"), None),
        P(("groups", "dp"), None),
    )
    return jax.shard_map(
        per_device, mesh=mesh, in_specs=placed, out_specs=P(("groups", "dp"), None), check_vma=False
    )
```

```python
import functools
import math

import jax
import jax.numpy as jnp
from jax import lax
from jax.experimental import pallas as pl
from jax.experimental.pallas import tpu as pltpu
from jax.sharding import PartitionSpec as P

H = 64
KVH = 4
DH = 128
TOP = 8
F32 = jnp.float32
BF16 = jnp.bfloat16


REDUCE = ((4, (0, 1, 2)), (4, (1, 2, 0)))
GATHER = ((3, (0, 1, 2)), (3, (1, 2, 0)), (2, (2, 0, 1)))


GROUP = 8
PAD = 16


def attend_kernel(core_ref, lengths_ref, q_ref, new_ref, cache_ref, out_ref, cache, q_rows, out_rows, new_rows, sems):
    rows = q_ref.shape[0]
    heads = q_ref.shape[1] // DH
    per_group = heads // KVH
    span, width = cache_ref.shape[2:]
    scale = 1.0 / math.sqrt(DH)

    def copy(side, at):
        part = pl.ds(at * GROUP, GROUP)
        return pltpu.make_async_copy(cache_ref.at[side, part], cache.at[side, part, pl.ds(0, span)], sems.at[side, at])

    for at in range(rows // GROUP):
        copy(0, at).start()
        copy(1, at).start()
    new_rows[...] = new_ref[...].astype(F32)
    for h in range(heads):
        q_rows[h * rows : (h + 1) * rows, :] = q_ref[:, h * DH : (h + 1) * DH].astype(F32)

    position = lax.broadcasted_iota(jnp.int32, (span + PAD, heads), 0)
    row_group = lax.broadcasted_iota(jnp.int32, (heads, width), 0) // per_group
    lane_group = lax.broadcasted_iota(jnp.int32, (heads, width), 1) // DH
    own_lanes = row_group == lane_group

    @pl.loop(0, rows // GROUP)
    def _(at):
        copy(0, at).wait()
        copy(1, at).wait()
        scores, probs = [], []
        for i in range(GROUP):
            t = at * GROUP + i
            for side in range(2):
                cache[side, t, span:, :] = jnp.broadcast_to(new_rows[side, pl.ds(t, 1), :], (PAD, width)).astype(BF16)
            query = q_rows[pl.ds(t, heads, stride=rows), :]
            spread = jnp.where(own_lanes, jnp.concatenate([query] * KVH, axis=1), 0.0).astype(BF16)
            scores.append(
                lax.dot_general(cache[0, t], spread, (((1,), (1,)), ((), ())), preferred_element_type=F32)
            )
        for i in range(GROUP):
            live = (position < lengths_ref[at * GROUP + i]) | (position == span)
            score = jnp.where(live, scores[i] * scale, -1e30)
            weights = jnp.exp(score - jnp.max(score, axis=0, keepdims=True))
            probs.append((weights * (1.0 / jnp.sum(weights, axis=0, keepdims=True))).astype(BF16))
        for i in range(GROUP):
            t = at * GROUP + i
            values = lax.dot_general(probs[i], cache[1, t], (((0,), (0,)), ((), ())), preferred_element_type=F32)
            for g in range(KVH):
                out_rows[pl.ds(g * per_group * rows + t, per_group, stride=rows), :] = values[
                    g * per_group : (g + 1) * per_group, g * DH : (g + 1) * DH
                ]

    chips = out_ref.shape[0]
    per_chip = heads // chips
    for side in range(2):

        @pl.when(core_ref[0] == side)
        def _():
            for e in range(chips):
                for i in range(per_chip):
                    h = e * per_chip + (i + side * (per_chip // 2)) % per_chip
                    out_ref[e, :, i * DH : (i + 1) * DH] = out_rows[h * rows : (h + 1) * rows, :].astype(BF16)


def attend(core, queries, new_kv, cache_kv, lengths, chips):
    rows, features = queries.shape
    sides, _, span, width = cache_kv.shape
    vmem = pl.BlockSpec(memory_space=pltpu.VMEM)
    smem = pl.BlockSpec(memory_space=pltpu.SMEM)
    return pl.pallas_call(
        attend_kernel,
        out_shape=jax.ShapeDtypeStruct((chips, rows, features // chips), BF16),
        in_specs=[smem, smem, vmem, vmem, pl.BlockSpec(memory_space=pl.ANY)],
        out_specs=vmem,
        scratch_shapes=[
            pltpu.VMEM((sides, rows, span + PAD, width), BF16),
            pltpu.VMEM((features // DH * rows, DH), F32),
            pltpu.VMEM((features // DH * rows, DH), F32),
            pltpu.VMEM((2, rows, width), F32),
            pltpu.SemaphoreType.DMA((2, rows // GROUP)),
        ],
        compiler_params=pltpu.CompilerParams(vmem_limit_bytes=58 << 20),
        cost_estimate=pl.CostEstimate(flops=4 * rows * features * span, bytes_accessed=2 * cache_kv.size, transcendentals=rows * features),
    )(core, lengths, queries, new_kv, cache_kv)


P_TILE = 512


def spans(chunks, width):
    at = 0
    for eighths, order in chunks:
        size = width * eighths // 8
        yield at, size, order
        at += size


def octants(order, half):
    size = half // 4
    for place in range(8):
        base = sum((place >> (2 - step) & 1) << (2 - order[step]) for step in range(3))
        at = place % 4 * size
        yield place // 4, slice(at, at + size), slice(base * size, (base + 1) * size)


def project_kernel(order, index_ref, blocks_ref, own_ref, other_ref, keep_ref, send_ref, ordered):
    chips, rows, features = blocks_ref.shape
    half = features // 2
    for k in range(chips):
        ordered[k * rows : (k + 1) * rows, :] = blocks_ref[index_ref[k]]
    for at in range(0, keep_ref.shape[1], P_TILE):
        lanes = slice(at, at + P_TILE)
        total = jnp.dot(ordered[:, :half], own_ref[:, lanes], preferred_element_type=F32)
        total = total + jnp.dot(ordered[:, half:], other_ref[:, lanes], preferred_element_type=F32)
        for to, here, where in octants(order, keep_ref.shape[0]):
            (keep_ref, send_ref)[to][here, lanes] = total[where].astype(BF16)


def whole(shape):
    return pl.BlockSpec(shape, lambda s: (0,) * len(shape))


def project(span, index, blocks, own, other):
    chips, rows, features = blocks.shape
    depth = own.shape[0]
    first, size, order = span
    weights = pl.BlockSpec((depth, size), lambda s: (0, first // size))
    half = (chips * rows // 2, size)
    return pl.pallas_call(
        functools.partial(project_kernel, order),
        out_shape=[jax.ShapeDtypeStruct(half, BF16)] * 2,
        grid=(1,),
        in_specs=[
            pl.BlockSpec(memory_space=pltpu.SMEM),
            whole(blocks.shape),
            weights,
            weights,
        ],
        out_specs=[whole(half)] * 2,
        scratch_shapes=[pltpu.VMEM((chips * rows, features), BF16)],
        compiler_params=pltpu.CompilerParams(vmem_limit_bytes=16 << 20),
        cost_estimate=pl.CostEstimate(flops=2 * blocks.size * size, bytes_accessed=4 * depth * size, transcendentals=0),
    )(index, blocks, own, other)


def bring_kernel(after_ref, *refs):
    count = len(refs) // 2
    sems = refs[-1]
    copies = [pltpu.make_async_copy(refs[i], refs[count + i], sems.at[i]) for i in range(count)]
    for copy in copies:
        copy.start()
    for copy in copies:
        copy.wait()


def bring(after, arrays):
    space = pl.BlockSpec(memory_space=pl.ANY)
    return pl.pallas_call(
        bring_kernel,
        out_shape=[jax.ShapeDtypeStruct(a.shape, a.dtype) for a in arrays],
        in_specs=[space] * (1 + len(arrays)),
        out_specs=[pl.BlockSpec(memory_space=pltpu.VMEM)] * len(arrays),
        scratch_shapes=[pltpu.SemaphoreType.DMA((len(arrays),))],
        compiler_params=pltpu.CompilerParams(vmem_limit_bytes=2 << 20),
        cost_estimate=pl.CostEstimate(flops=0, bytes_accessed=2 * sum(a.size for a in arrays), transcendentals=0),
    )(after, *arrays)


F_TILE = 256
N_TILE = 512


def activate(tokens_ref, gate_ref, up_ref, active_ref):
    for at in range(0, gate_ref.shape[1], F_TILE):
        lanes = slice(at, at + F_TILE)
        gate_part = jnp.dot(tokens_ref[...], gate_ref[:, lanes], preferred_element_type=F32)
        up_part = jnp.dot(tokens_ref[...], up_ref[:, lanes], preferred_element_type=F32)
        active_ref[:, lanes] = (gate_part / (1.0 + jnp.exp(-gate_part)) * up_part).astype(BF16)


def first_kernel(chip_ref, *refs):
    pieces, (gate_ref, up_ref, tokens_ref, active_ref, weights_ref) = refs[:-5], refs[-5:]
    half = pieces[0].shape[0]
    for c, (at, size, order) in enumerate(spans(GATHER, tokens_ref.shape[1])):
        for side, here, where in octants(order, half):
            tokens_ref[where, at : at + size] = pieces[2 * c + side][here, :size]
    chunk = GATHER[0][0] * tokens_ref.shape[1] // 8
    first, chips = chip_ref[0], chip_ref[1]
    lane = lax.broadcasted_iota(jnp.int32, (half, pieces[0].shape[1] - chunk), 1)
    mine = (lane == first) | (lane == first + chips) | (lane == first + 2 * chips)
    for side in range(2):
        weights_ref[side * half : (side + 1) * half, :] = jnp.sum(
            jnp.where(mine, pieces[side][:, chunk:].astype(F32), 0.0), axis=1, keepdims=True
        )
    activate(tokens_ref, gate_ref, up_ref, active_ref)


def down_kernel(order, after_ref, active0, active1, weights_ref, down0, down1, keep_ref, send_ref):
    for at in range(0, keep_ref.shape[1], N_TILE):
        lanes = slice(at, at + N_TILE)
        total = jnp.dot(active0[...], down0[:, lanes], preferred_element_type=F32)
        total = total + jnp.dot(active1[...], down1[:, lanes], preferred_element_type=F32)
        total = total * weights_ref[...]
        for to, here, where in octants(order, keep_ref.shape[0]):
            (keep_ref, send_ref)[to][here, lanes] = total[where].astype(BF16)


def experts(chip, pieces, gates, ups, downs):
    half = pieces[0].shape[0]
    rows = 2 * half
    width, hidden = gates[0].shape
    params = pltpu.CompilerParams(vmem_limit_bytes=20 << 20)
    cost = pl.CostEstimate(flops=4 * rows * width * hidden, bytes_accessed=4 * width * hidden, transcendentals=rows * hidden)
    vmem = pl.BlockSpec(memory_space=pltpu.VMEM)
    active = jax.ShapeDtypeStruct((rows, hidden), BF16)
    tokens, active0, weights = pl.pallas_call(
        first_kernel,
        out_shape=[jax.ShapeDtypeStruct((rows, width), BF16), active, jax.ShapeDtypeStruct((rows, 1), F32)],
        in_specs=[pl.BlockSpec(memory_space=pltpu.SMEM)] + [vmem] * (len(pieces) + 2),
        out_specs=[vmem] * 3,
        compiler_params=params,
        cost_estimate=cost,
    )(chip, *pieces, gates[0], ups[0])
    active1 = pl.pallas_call(
        activate,
        out_shape=active,
        in_specs=[vmem] * 3,
        out_specs=vmem,
        compiler_params=params,
        cost_estimate=cost,
    )(tokens, gates[1], ups[1])
    results = []
    for first, size, order in spans(REDUCE, width):
        block = pl.BlockSpec((hidden, size), functools.partial(lambda s, index: (0, index), index=first // size))
        results += pl.pallas_call(
            functools.partial(down_kernel, order),
            out_shape=[jax.ShapeDtypeStruct((half, size), BF16)] * 2,
            grid=(1,),
            in_specs=[pl.BlockSpec(memory_space=pl.ANY), whole((rows, hidden)), whole((rows, hidden)), whole((rows, 1))]
            + [block, block],
            out_specs=[whole((half, size))] * 2,
            compiler_params=params,
            cost_estimate=pl.CostEstimate(flops=4 * rows * size * hidden, bytes_accessed=4 * size * hidden, transcendentals=0),
        )(results[-1] if results else active1, active0, active1, weights, *downs)
    return results


def normalize(hidden_state, norm_gain):
    values = [part.astype(F32) for part in hidden_state]
    square = sum(jnp.sum(part * part, axis=-1, keepdims=True) for part in values)
    scale = lax.rsqrt(square / norm_gain.size + 1e-06)
    gains = [norm_gain[at : at + size] for at, size, _ in spans(REDUCE, norm_gain.size)]
    return [(part * scale * gain).astype(BF16) for part, gain in zip(values, gains)]


def step_bits(devices, order=(0, 1, 2)):
    even = [1 << i for i in range(1, devices.bit_length() - 1)]
    odd = [even[i] for i in (2, 0, 1)] + even[3:]
    return [[bits[i] for i in order] + bits[3:] for bits in (even, odd)]


def swap_step(step, order, devices):
    orders = step_bits(devices, order)
    return [(i, i ^ orders[i & 1][step]) for i in range(devices)]


def reduce_slots(pieces, devices):
    steps = devices.bit_length() - 2
    kept, sent = list(pieces[::2]), list(pieces[1::2])
    for step in range(steps):
        for c, (_, order) in enumerate(REDUCE):
            came = lax.ppermute(sent[c], "dp", swap_step(step, order, devices))
            kept[c] = kept[c].astype(F32) + came.astype(F32)
            half = kept[c].shape[0] // 2
            if step < steps - 1:
                sent[c] = kept[c][half:].astype(BF16)
                kept[c] = kept[c][:half]
    return kept


def gather_slots(own, devices):
    own = list(own)
    steps = devices.bit_length() - 2
    pieces = []
    for step in reversed(range(steps)):
        for c, (_, order) in enumerate(GATHER):
            came = lax.ppermute(own[c], "dp", swap_step(step, order, devices))
            if step == 0:
                pieces += [own[c], came]
            else:
                own[c] = jnp.concatenate([own[c], came], axis=0)
    return pieces


def per_device(
    residual,
    queries,
    new_kv,
    cache_kv,
    lengths,
    out_weight,
    norm_gain,
    w_gate,
    w_up,
    w_down,
    expert_ids,
    combine_weights,
):
    rows, width = residual.shape
    devices = lax.axis_size("dp")
    chips = devices // 2
    me = lax.axis_index("dp")
    core = me % 2
    chip = me // 2
    steps = devices.bit_length() - 2
    core_swap = [(i, i ^ 1) for i in range(devices)]
    core_groups = [[2 * i + c for i in range(chips)] for c in range(2)]

    out_other = lax.ppermute(out_weight, "dp", core_swap)
    gate_other = lax.ppermute(w_gate[0], "dp", core_swap)
    up_other = lax.ppermute(w_up[0], "dp", core_swap)
    down_other = lax.ppermute(w_down[0], "dp", core_swap)

    attn_out = attend(core[None], queries, new_kv, cache_kv, lengths, chips)
    blocks = lax.all_to_all(
        attn_out, "dp", split_axis=0, concat_axis=0, axis_index_groups=core_groups, tiled=True
    )

    orders = step_bits(devices)
    slot = jnp.arange(chips, dtype=jnp.int32)
    offset = jnp.zeros_like(slot)
    for step in range(steps):
        here = jnp.where(core == 0, orders[0][step], orders[1][step]) // 2
        offset = offset + here * ((slot >> (steps - 1 - step)) & 1)
    cuts = list(spans(REDUCE, width))
    partial = []
    for span in cuts:
        partial += project(span, chip ^ offset, blocks, out_weight, out_other)
    projected = reduce_slots(partial, devices)
    hidden_state = [
        (residual[:, at : at + size].astype(F32) + add).astype(BF16) for (at, size, _), add in zip(cuts, projected)
    ]
    normed = normalize(hidden_state, norm_gain)

    picks = expert_ids[:, :, None] == jnp.arange(chips, dtype=jnp.int32)
    mix = jnp.sum(jnp.where(picks, combine_weights[:, :, None], 0.0), axis=1)
    mix_hi = mix.astype(BF16)
    mix_mid = (mix - mix_hi.astype(F32)).astype(BF16)
    mix_low = (mix - mix_hi.astype(F32) - mix_mid.astype(F32)).astype(BF16)
    extra = jnp.concatenate([mix_hi, mix_mid, mix_low], axis=1)
    extra = jnp.pad(extra, ((0, 0), (0, -extra.shape[1] % 128)))
    normed, gate_other, up_other, down_other = lax.optimization_barrier((normed, gate_other, up_other, down_other))
    normed = jnp.concatenate(normed, axis=1)
    normed = [normed[:, at : at + size] for at, size, _ in spans(GATHER, width)]
    normed[0] = jnp.concatenate([normed[0], extra], axis=1)
    pieces = gather_slots(normed, devices)
    gate_other, up_other, down_other = bring(pieces[-2], (gate_other, up_other, down_other))
    place = jnp.stack([chip, jnp.int32(chips)])
    outs = experts(place, pieces, (w_gate[0], gate_other), (w_up[0], up_other), (w_down[0], down_other))
    mixture = reduce_slots(outs, devices)
    return jnp.concatenate(
        [(part.astype(F32) + add).astype(BF16) for part, add in zip(hidden_state, mixture)], axis=1
    )


def solution(mesh):
    placed = (
        P(("groups", "dp"), None),
        P(("groups", "dp"), None),
        P(None, ("groups", "dp"), None),
        P(None, ("groups", "dp"), None, None),
        P(("groups", "dp")),
        P("dp", None),
        P(),
        P("dp", None, None),
        P("dp", None, None),
        P("dp", None, None),
        P(("groups", "dp"), None),
        P(("groups", "dp"), None),
    )
    return jax.shard_map(
        per_device, mesh=mesh, in_specs=placed, out_specs=P(("groups", "dp"), None), check_vma=False
    )
```

```python
import functools
import math

import jax
import jax.numpy as jnp
from jax import lax
from jax.experimental import pallas as pl
from jax.experimental.pallas import tpu as pltpu
from jax.sharding import PartitionSpec as P

H = 64
KVH = 4
DH = 128
TOP = 8
F32 = jnp.float32
BF16 = jnp.bfloat16


REDUCE = ((4, (0, 1, 2)), (4, (1, 2, 0)))
GATHER = ((3, (0, 1, 2)), (3, (1, 0, 2)), (2, (2, 0, 1)))


GROUP = 8
PAD = 16


def attend_kernel(core_ref, lengths_ref, q_ref, new_ref, cache_ref, out_ref, cache, q_rows, out_rows, new_rows, sems):
    rows = q_ref.shape[0]
    heads = q_ref.shape[1] // DH
    per_group = heads // KVH
    span, width = cache_ref.shape[2:]
    scale = 1.0 / math.sqrt(DH)

    def copy(side, at):
        part = pl.ds(at * GROUP, GROUP)
        return pltpu.make_async_copy(cache_ref.at[side, part], cache.at[side, part, pl.ds(0, span)], sems.at[side, at])

    for at in range(rows // GROUP):
        copy(0, at).start()
        copy(1, at).start()
    new_rows[...] = new_ref[...].astype(F32)
    for h in range(heads):
        q_rows[h * rows : (h + 1) * rows, :] = q_ref[:, h * DH : (h + 1) * DH].astype(F32)

    position = lax.broadcasted_iota(jnp.int32, (span + PAD, heads), 0)
    row_group = lax.broadcasted_iota(jnp.int32, (heads, width), 0) // per_group
    lane_group = lax.broadcasted_iota(jnp.int32, (heads, width), 1) // DH
    own_lanes = row_group == lane_group

    @pl.loop(0, rows // GROUP)
    def _(at):
        copy(0, at).wait()
        copy(1, at).wait()
        scores, probs = [], []
        for i in range(GROUP):
            t = at * GROUP + i
            for side in range(2):
                cache[side, t, span:, :] = jnp.broadcast_to(new_rows[side, pl.ds(t, 1), :], (PAD, width)).astype(BF16)
            query = q_rows[pl.ds(t, heads, stride=rows), :]
            spread = jnp.where(own_lanes, jnp.concatenate([query] * KVH, axis=1), 0.0).astype(BF16)
            scores.append(
                lax.dot_general(cache[0, t], spread, (((1,), (1,)), ((), ())), preferred_element_type=F32)
            )
        for i in range(GROUP):
            live = (position < lengths_ref[at * GROUP + i]) | (position == span)
            score = jnp.where(live, scores[i] * scale, -1e30)
            weights = jnp.exp(score - jnp.max(score, axis=0, keepdims=True))
            probs.append((weights * (1.0 / jnp.sum(weights, axis=0, keepdims=True))).astype(BF16))
        for i in range(GROUP):
            t = at * GROUP + i
            values = lax.dot_general(probs[i], cache[1, t], (((0,), (0,)), ((), ())), preferred_element_type=F32)
            for g in range(KVH):
                out_rows[pl.ds(g * per_group * rows + t, per_group, stride=rows), :] = values[
                    g * per_group : (g + 1) * per_group, g * DH : (g + 1) * DH
                ]

    chips = out_ref.shape[0]
    per_chip = heads // chips
    for side in range(2):

        @pl.when(core_ref[0] == side)
        def _():
            for e in range(chips):
                for i in range(per_chip):
                    h = e * per_chip + (i + side * (per_chip // 2)) % per_chip
                    out_ref[e, :, i * DH : (i + 1) * DH] = out_rows[h * rows : (h + 1) * rows, :].astype(BF16)


def attend(core, queries, new_kv, cache_kv, lengths, chips):
    rows, features = queries.shape
    sides, _, span, width = cache_kv.shape
    vmem = pl.BlockSpec(memory_space=pltpu.VMEM)
    smem = pl.BlockSpec(memory_space=pltpu.SMEM)
    return pl.pallas_call(
        attend_kernel,
        out_shape=jax.ShapeDtypeStruct((chips, rows, features // chips), BF16),
        in_specs=[smem, smem, vmem, vmem, pl.BlockSpec(memory_space=pl.ANY)],
        out_specs=vmem,
        scratch_shapes=[
            pltpu.VMEM((sides, rows, span + PAD, width), BF16),
            pltpu.VMEM((features // DH * rows, DH), F32),
            pltpu.VMEM((features // DH * rows, DH), F32),
            pltpu.VMEM((2, rows, width), F32),
            pltpu.SemaphoreType.DMA((2, rows // GROUP)),
        ],
        compiler_params=pltpu.CompilerParams(vmem_limit_bytes=58 << 20),
        cost_estimate=pl.CostEstimate(flops=4 * rows * features * span, bytes_accessed=2 * cache_kv.size, transcendentals=rows * features),
    )(core, lengths, queries, new_kv, cache_kv)


P_TILE = 1024


def spans(chunks, width):
    at = 0
    for eighths, order in chunks:
        size = width * eighths // 8
        yield at, size, order
        at += size


def octants(order, half):
    size = half // 4
    for place in range(8):
        base = sum((place >> (2 - step) & 1) << (2 - order[step]) for step in range(3))
        at = place % 4 * size
        yield place // 4, slice(at, at + size), slice(base * size, (base + 1) * size)


def project_kernel(order, index_ref, blocks_ref, own_ref, other_ref, keep_ref, send_ref, ordered):
    chips, rows, features = blocks_ref.shape
    half = features // 2
    for k in range(chips):
        ordered[k * rows : (k + 1) * rows, :] = blocks_ref[index_ref[k]]
    for at in range(0, keep_ref.shape[1], P_TILE):
        lanes = slice(at, at + P_TILE)
        total = jnp.dot(ordered[:, :half], own_ref[:, lanes], preferred_element_type=F32)
        total = total + jnp.dot(ordered[:, half:], other_ref[:, lanes], preferred_element_type=F32)
        for to, here, where in octants(order, keep_ref.shape[0]):
            (keep_ref, send_ref)[to][here, lanes] = total[where].astype(BF16)


def whole(shape):
    return pl.BlockSpec(shape, lambda s: (0,) * len(shape))


def project(span, index, blocks, own, other):
    chips, rows, features = blocks.shape
    depth = own.shape[0]
    first, size, order = span
    weights = pl.BlockSpec((depth, size), lambda s: (0, first // size))
    half = (chips * rows // 2, size)
    return pl.pallas_call(
        functools.partial(project_kernel, order),
        out_shape=[jax.ShapeDtypeStruct(half, BF16)] * 2,
        grid=(1,),
        in_specs=[
            pl.BlockSpec(memory_space=pltpu.SMEM),
            whole(blocks.shape),
            weights,
            weights,
        ],
        out_specs=[whole(half)] * 2,
        scratch_shapes=[pltpu.VMEM((chips * rows, features), BF16)],
        compiler_params=pltpu.CompilerParams(vmem_limit_bytes=16 << 20),
        cost_estimate=pl.CostEstimate(flops=2 * blocks.size * size, bytes_accessed=4 * depth * size, transcendentals=0),
    )(index, blocks, own, other)


def bring_kernel(after_ref, *refs):
    count = len(refs) // 2
    sems = refs[-1]
    copies = [pltpu.make_async_copy(refs[i], refs[count + i], sems.at[i]) for i in range(count)]
    for copy in copies:
        copy.start()
    for copy in copies:
        copy.wait()


def bring(after, arrays):
    space = pl.BlockSpec(memory_space=pl.ANY)
    return pl.pallas_call(
        bring_kernel,
        out_shape=[jax.ShapeDtypeStruct(a.shape, a.dtype) for a in arrays],
        in_specs=[space] * (1 + len(arrays)),
        out_specs=[pl.BlockSpec(memory_space=pltpu.VMEM)] * len(arrays),
        scratch_shapes=[pltpu.SemaphoreType.DMA((len(arrays),))],
        compiler_params=pltpu.CompilerParams(vmem_limit_bytes=2 << 20),
        cost_estimate=pl.CostEstimate(flops=0, bytes_accessed=2 * sum(a.size for a in arrays), transcendentals=0),
    )(after, *arrays)


F_TILE = 256
N_TILE = 512


def activate(tokens_ref, gate_ref, up_ref, active_ref):
    for at in range(0, gate_ref.shape[1], F_TILE):
        lanes = slice(at, at + F_TILE)
        gate_part = jnp.dot(tokens_ref[...], gate_ref[:, lanes], preferred_element_type=F32)
        up_part = jnp.dot(tokens_ref[...], up_ref[:, lanes], preferred_element_type=F32)
        active_ref[:, lanes] = (gate_part / (1.0 + jnp.exp(-gate_part)) * up_part).astype(BF16)


def first_kernel(chip_ref, *refs):
    pieces, (gate_ref, up_ref, tokens_ref, active_ref, weights_ref) = refs[:-5], refs[-5:]
    half = pieces[0].shape[0]
    for c, (at, size, order) in enumerate(spans(GATHER, tokens_ref.shape[1])):
        for side, here, where in octants(order, half):
            tokens_ref[where, at : at + size] = pieces[2 * c + side][here, :size]
    chunk = GATHER[0][0] * tokens_ref.shape[1] // 8
    first, chips = chip_ref[0], chip_ref[1]
    lane = lax.broadcasted_iota(jnp.int32, (half, pieces[0].shape[1] - chunk), 1)
    mine = (lane == first) | (lane == first + chips) | (lane == first + 2 * chips)
    for side in range(2):
        weights_ref[side * half : (side + 1) * half, :] = jnp.sum(
            jnp.where(mine, pieces[side][:, chunk:].astype(F32), 0.0), axis=1, keepdims=True
        )
    activate(tokens_ref, gate_ref, up_ref, active_ref)


def down_kernel(order, after_ref, active0, active1, weights_ref, down0, down1, keep_ref, send_ref):
    for at in range(0, keep_ref.shape[1], N_TILE):
        lanes = slice(at, at + N_TILE)
        total = jnp.dot(active0[...], down0[:, lanes], preferred_element_type=F32)
        total = total + jnp.dot(active1[...], down1[:, lanes], preferred_element_type=F32)
        total = total * weights_ref[...]
        for to, here, where in octants(order, keep_ref.shape[0]):
            (keep_ref, send_ref)[to][here, lanes] = total[where].astype(BF16)


def experts(chip, pieces, gates, ups, downs):
    half = pieces[0].shape[0]
    rows = 2 * half
    width, hidden = gates[0].shape
    params = pltpu.CompilerParams(vmem_limit_bytes=20 << 20)
    cost = pl.CostEstimate(flops=4 * rows * width * hidden, bytes_accessed=4 * width * hidden, transcendentals=rows * hidden)
    vmem = pl.BlockSpec(memory_space=pltpu.VMEM)
    active = jax.ShapeDtypeStruct((rows, hidden), BF16)
    tokens, active0, weights = pl.pallas_call(
        first_kernel,
        out_shape=[jax.ShapeDtypeStruct((rows, width), BF16), active, jax.ShapeDtypeStruct((rows, 1), F32)],
        in_specs=[pl.BlockSpec(memory_space=pltpu.SMEM)] + [vmem] * (len(pieces) + 2),
        out_specs=[vmem] * 3,
        compiler_params=params,
        cost_estimate=cost,
    )(chip, *pieces, gates[0], ups[0])
    active1 = pl.pallas_call(
        activate,
        out_shape=active,
        in_specs=[vmem] * 3,
        out_specs=vmem,
        compiler_params=params,
        cost_estimate=cost,
    )(tokens, gates[1], ups[1])
    results = []
    for first, size, order in spans(REDUCE, width):
        block = pl.BlockSpec((hidden, size), functools.partial(lambda s, index: (0, index), index=first // size))
        results += pl.pallas_call(
            functools.partial(down_kernel, order),
            out_shape=[jax.ShapeDtypeStruct((half, size), BF16)] * 2,
            grid=(1,),
            in_specs=[pl.BlockSpec(memory_space=pl.ANY), whole((rows, hidden)), whole((rows, hidden)), whole((rows, 1))]
            + [block, block],
            out_specs=[whole((half, size))] * 2,
            compiler_params=params,
            cost_estimate=pl.CostEstimate(flops=4 * rows * size * hidden, bytes_accessed=4 * size * hidden, transcendentals=0),
        )(results[-1] if results else active1, active0, active1, weights, *downs)
    return results


def normalize(hidden_state, norm_gain):
    values = [part.astype(F32) for part in hidden_state]
    square = sum(jnp.sum(part * part, axis=-1, keepdims=True) for part in values)
    scale = lax.rsqrt(square / norm_gain.size + 1e-06)
    gains = [norm_gain[at : at + size] for at, size, _ in spans(REDUCE, norm_gain.size)]
    return [(part * scale * gain).astype(BF16) for part, gain in zip(values, gains)]


def step_bits(devices, order=(0, 1, 2)):
    even = [1 << i for i in range(1, devices.bit_length() - 1)]
    odd = [even[i] for i in (2, 0, 1)] + even[3:]
    return [[bits[i] for i in order] + bits[3:] for bits in (even, odd)]


def swap_step(step, order, devices):
    orders = step_bits(devices, order)
    return [(i, i ^ orders[i & 1][step]) for i in range(devices)]


def reduce_slots(pieces, devices):
    steps = devices.bit_length() - 2
    kept, sent = list(pieces[::2]), list(pieces[1::2])
    for step in range(steps):
        for c, (_, order) in enumerate(REDUCE):
            came = lax.ppermute(sent[c], "dp", swap_step(step, order, devices))
            kept[c] = kept[c].astype(F32) + came.astype(F32)
            half = kept[c].shape[0] // 2
            if step < steps - 1:
                sent[c] = kept[c][half:].astype(BF16)
                kept[c] = kept[c][:half]
    return kept


def gather_slots(own, devices):
    own = list(own)
    steps = devices.bit_length() - 2
    pieces = []
    for step in reversed(range(steps)):
        for c, (_, order) in enumerate(GATHER):
            came = lax.ppermute(own[c], "dp", swap_step(step, order, devices))
            if step == 0:
                pieces += [own[c], came]
            else:
                own[c] = jnp.concatenate([own[c], came], axis=0)
    return pieces


def per_device(
    residual,
    queries,
    new_kv,
    cache_kv,
    lengths,
    out_weight,
    norm_gain,
    w_gate,
    w_up,
    w_down,
    expert_ids,
    combine_weights,
):
    rows, width = residual.shape
    devices = lax.axis_size("dp")
    chips = devices // 2
    me = lax.axis_index("dp")
    core = me % 2
    chip = me // 2
    steps = devices.bit_length() - 2
    core_swap = [(i, i ^ 1) for i in range(devices)]
    core_groups = [[2 * i + c for i in range(chips)] for c in range(2)]

    out_other = lax.ppermute(out_weight, "dp", core_swap)
    gate_other = lax.ppermute(w_gate[0], "dp", core_swap)
    up_other = lax.ppermute(w_up[0], "dp", core_swap)
    down_other = lax.ppermute(w_down[0], "dp", core_swap)

    attn_out = attend(core[None], queries, new_kv, cache_kv, lengths, chips)
    blocks = lax.all_to_all(
        attn_out, "dp", split_axis=0, concat_axis=0, axis_index_groups=core_groups, tiled=True
    )

    orders = step_bits(devices)
    slot = jnp.arange(chips, dtype=jnp.int32)
    offset = jnp.zeros_like(slot)
    for step in range(steps):
        here = jnp.where(core == 0, orders[0][step], orders[1][step]) // 2
        offset = offset + here * ((slot >> (steps - 1 - step)) & 1)
    cuts = list(spans(REDUCE, width))
    partial = []
    for span in cuts:
        partial += project(span, chip ^ offset, blocks, out_weight, out_other)
    projected = reduce_slots(partial, devices)
    hidden_state = [
        (residual[:, at : at + size].astype(F32) + add).astype(BF16) for (at, size, _), add in zip(cuts, projected)
    ]
    normed = normalize(hidden_state, norm_gain)

    picks = expert_ids[:, :, None] == jnp.arange(chips, dtype=jnp.int32)
    mix = jnp.sum(jnp.where(picks, combine_weights[:, :, None], 0.0), axis=1)
    mix_hi = mix.astype(BF16)
    mix_mid = (mix - mix_hi.astype(F32)).astype(BF16)
    mix_low = (mix - mix_hi.astype(F32) - mix_mid.astype(F32)).astype(BF16)
    extra = jnp.concatenate([mix_hi, mix_mid, mix_low], axis=1)
    extra = jnp.pad(extra, ((0, 0), (0, -extra.shape[1] % 128)))
    normed, gate_other, up_other, down_other = lax.optimization_barrier((normed, gate_other, up_other, down_other))
    normed = jnp.concatenate(normed, axis=1)
    normed = [normed[:, at : at + size] for at, size, _ in spans(GATHER, width)]
    normed[0] = jnp.concatenate([normed[0], extra], axis=1)
    pieces = gather_slots(normed, devices)
    gate_other, up_other, down_other = bring(pieces[-2], (gate_other, up_other, down_other))
    place = jnp.stack([chip, jnp.int32(chips)])
    outs = experts(place, pieces, (w_gate[0], gate_other), (w_up[0], up_other), (w_down[0], down_other))
    mixture = reduce_slots(outs, devices)
    return jnp.concatenate(
        [(part.astype(F32) + add).astype(BF16) for part, add in zip(hidden_state, mixture)], axis=1
    )


def solution(mesh):
    placed = (
        P(("groups", "dp"), None),
        P(("groups", "dp"), None),
        P(None, ("groups", "dp"), None),
        P(None, ("groups", "dp"), None, None),
        P(("groups", "dp")),
        P("dp", None),
        P(),
        P("dp", None, None),
        P("dp", None, None),
        P("dp", None, None),
        P(("groups", "dp"), None),
        P(("groups", "dp"), None),
    )
    return jax.shard_map(
        per_device, mesh=mesh, in_specs=placed, out_specs=P(("groups", "dp"), None), check_vma=False
    )
```
